256 devices in a mesh: dom: 16 (over y, z_hi), row: 16 (over x, z_lo, core).
Axes of the slice: x: 4, y: 4, z: 8 (z_hi: 4, z_lo: 2; z = z_hi * 2 + z_lo), core: 2. Of those that a mesh axis runs over, the one named last changes fastest.
Arguments:
- left_emb: float32 [32768, 400], P(('dom', 'row')), may hold values from -1.5 to 1.5
- left_state: float32 [32768], P(('dom', 'row')), may hold values from 0.05 to 1
- right_emb: float32 [32768, 400], P(('dom', 'row')), may hold values from -1.5 to 1.5
- right_state: float32 [32768], P(('dom', 'row')), may hold values from 0.05 to 1
- rel_diag: float32 [16, 400], replicated, may hold values from -4 to 4
- edge_src: int32 [2, 262144], P(None, ('dom', 'row')), may hold values from 0 to 2047
- edge_rel: int32 [2, 262144], P(None, ('dom', 'row')), may hold values from 0 to 15
- edge_dst: int32 [2, 262144], P(None, ('dom', 'row')), may hold values from 0 to 2047
- neg_rows: int32 [2, 256, 128], P(None, ('dom', 'row')), may hold values from 0 to 2047
Outputs:
- left_table: float32 [32768, 400], P(('dom', 'row'))
- left_accum: float32 [32768], P(('dom', 'row'))
- right_table: float32 [32768, 400], P(('dom', 'row'))
- right_accum: float32 [32768], P(('dom', 'row'))
- relation_grad: float32 [16, 400], replicated
The draws below stay inside these ranges and needn't reach their ends.
All inputs are finite; a program needn't handle non-finite values.
Results may differ from the reference program's by a relative error of at most 0.0021.
Values may be sent and summed in bfloat16 or wider, within the bound.
A program may use at most 64 MiB of HBM per device.

```python
import math
import jax
import jax.numpy as jnp
from jax import lax

D = 400
RELS = 16
SPAN = 1024
UNIFORM = 128
ROUNDS = 2
SPANS_DEV = 1
PART = 2048
ENTS = 32768
EDGES = 262144
N_DOM = 16
N_ROW = 16
DEVICES = 256


def set_ends(entries, rng, low, largest):
    longest = entries.shape.index(max(entries.shape))
    spots = []
    for shift in (0, 1):
        where = [jax.random.randint(jax.random.fold_in(rng, axis), (), 0, length) for axis, length in enumerate(entries.shape)]
        where[longest] = (where[longest] + shift) % entries.shape[longest]
        spots.append(tuple(where))
    return entries.at[spots[0]].set(low).at[spots[1]].set(largest)


def shard_levels(own_key, dims, pieces, least, top_value):
    gain = 1.0
    for axis_at, parts in pieces:
        steps = jax.random.uniform(jax.random.fold_in(jax.random.fold_in(own_key, 6), axis_at), (parts,), jnp.float32, least / len(pieces), top_value / len(pieces))
        gain = gain * jnp.repeat(jnp.exp(steps), dims[axis_at] // parts).reshape((-1,) + (1,) * (len(dims) - 1 - axis_at))
    return gain


def centred(rng, dims, scale, limit, cuts=(), kind=jnp.bfloat16):
    loudness = shard_levels(rng, dims, cuts, -0.22, 0.18) if cuts else 1.0
    drawn = jax.random.normal(rng, dims, jnp.float32) * scale * loudness
    return jnp.minimum(jnp.maximum(drawn, -limit), limit).astype(kind)


def setup_inputs(seed: int = 0) -> dict:
    streams_of = jax.random.split(jax.random.key(seed), 10)
    left_emb = centred(streams_of[0], (ENTS, D), 0.25, 1.5, ((0, 256),), jnp.float32)
    left_state = jnp.clip(jnp.exp(math.log(1.0) - 2.9957323 * jax.random.uniform(streams_of[1], (ENTS,), jnp.float32) ** shard_levels(streams_of[1], (ENTS,), ((0, 256),), -0.2, 0.2)), 0.05, 1.0)
    right_emb = centred(streams_of[2], (ENTS, D), 0.25, 1.5, ((0, 256),), jnp.float32)
    right_state = jnp.clip(jnp.exp(math.log(1.0) - 2.9957323 * jax.random.uniform(streams_of[3], (ENTS,), jnp.float32) ** shard_levels(streams_of[3], (ENTS,), ((0, 256),), -0.2, 0.2)), 0.05, 1.0)
    rel_diag = centred(streams_of[4], (RELS, D), 1.0, 4.0, (), jnp.float32)
    edge_src = set_ends(jax.random.randint(streams_of[5], (ROUNDS, EDGES), 0, PART), jax.random.fold_in(streams_of[5], 1), 0, PART - 1).astype(jnp.int32)
    edge_rel = set_ends(jax.random.randint(streams_of[6], (ROUNDS, EDGES), 0, RELS), jax.random.fold_in(streams_of[6], 1), 0, RELS - 1).astype(jnp.int32)
    edge_dst = set_ends(jax.random.randint(streams_of[7], (ROUNDS, EDGES), 0, PART), jax.random.fold_in(streams_of[7], 1), 0, PART - 1).astype(jnp.int32)
    neg_rows = set_ends(jax.random.randint(streams_of[8], (ROUNDS, SPANS_DEV * DEVICES, UNIFORM), 0, PART), jax.random.fold_in(streams_of[8], 1), 0, PART - 1).astype(jnp.int32)
    return {"left_emb": left_emb, "left_state": left_state, "right_emb": right_emb, "right_state": right_state, "rel_diag": rel_diag, "edge_src": edge_src, "edge_rel": edge_rel, "edge_dst": edge_dst, "neg_rows": neg_rows}


STEP_SIZE = 0.1
EPSILON = 1e-10

def span_terms(left_rows, right_rows, neg_block, rel_rows, rel_ids):
    neg_count = SPAN - 1 + UNIFORM
    anchor = (left_rows.astype(jnp.float32) * rel_rows).astype(jnp.bfloat16)
    inner_scores = jnp.dot(anchor, right_rows.T, preferred_element_type=jnp.float32)
    outer_scores = jnp.dot(anchor, neg_block.T, preferred_element_type=jnp.float32)
    diagonal = jnp.eye(SPAN, dtype=bool)
    w_inner = jnp.where(diagonal, -jax.nn.sigmoid(-inner_scores), jax.nn.sigmoid(inner_scores) / neg_count).astype(jnp.bfloat16)
    w_outer = (jax.nn.sigmoid(outer_scores) / neg_count).astype(jnp.bfloat16)
    grad_anchor = jnp.dot(w_inner, right_rows, preferred_element_type=jnp.float32) + jnp.dot(w_outer, neg_block, preferred_element_type=jnp.float32)
    grad_dst = jnp.dot(w_inner.T, anchor, preferred_element_type=jnp.float32)
    grad_neg = jnp.dot(w_outer.T, anchor, preferred_element_type=jnp.float32)
    grad_src = grad_anchor * rel_rows
    grad_rel = jax.ops.segment_sum(grad_anchor * left_rows.astype(jnp.float32), rel_ids, num_segments=RELS)
    return (grad_src, grad_dst, grad_neg, grad_rel)

def adagrad(rows_in, state_in, grad_in):
    new_state = state_in + lax.optimization_barrier(jnp.mean(grad_in * grad_in, axis=-1))
    return (rows_in - STEP_SIZE * grad_in / (jnp.sqrt(new_state)[:, None] + EPSILON), new_state)

def reference(left_emb, left_state, right_emb, right_state, rel_diag, edge_src, edge_rel, edge_dst, neg_rows):
    half_dom = N_DOM // 2
    rel_total = jnp.zeros((RELS, D), jnp.float32)
    for round_idx in range(ROUNDS):
        left_low = left_emb.astype(jnp.bfloat16).reshape(N_DOM, PART, D)
        right_low = right_emb.astype(jnp.bfloat16).reshape(N_DOM, PART, D)
        src_all = edge_src[round_idx].reshape(N_DOM, N_ROW, SPANS_DEV, SPAN)
        rel_all = edge_rel[round_idx].reshape(N_DOM, N_ROW, SPANS_DEV, SPAN)
        dst_all = edge_dst[round_idx].reshape(N_DOM, N_ROW, SPANS_DEV, SPAN)
        neg_all = neg_rows[round_idx].reshape(N_DOM, N_ROW, SPANS_DEV, UNIFORM)
        shift_by = round_idx * half_dom

        def holder(holder_idx):
            left_slab = left_low[holder_idx]
            right_slab = right_low[(holder_idx + shift_by) % N_DOM]

            def device(totals, row_idx):
                acc_left, acc_right, acc_rel = totals
                term_left = jnp.zeros((PART, D), jnp.float32)
                term_right = jnp.zeros((PART, D), jnp.float32)
                for span_idx in range(SPANS_DEV):
                    sources = src_all[holder_idx, row_idx, span_idx]
                    rel_ids = rel_all[holder_idx, row_idx, span_idx]
                    targets = dst_all[holder_idx, row_idx, span_idx]
                    negatives = neg_all[holder_idx, row_idx, span_idx]
                    grad_src, grad_dst, grad_neg, grad_rel = span_terms(left_slab[sources], right_slab[targets], right_slab[negatives], rel_diag[rel_ids], rel_ids)
                    term_left = term_left.at[sources].add(grad_src)
                    term_right = term_right.at[targets].add(grad_dst).at[negatives].add(grad_neg)
                    acc_rel = acc_rel + grad_rel
                return ((acc_left + term_left, acc_right + term_right, acc_rel), None)
            start_totals = (jnp.zeros((PART, D), jnp.float32), jnp.zeros((PART, D), jnp.float32), jnp.zeros((RELS, D), jnp.float32))
            totals, _ = lax.scan(device, start_totals, jnp.arange(N_ROW, dtype=jnp.int32))
            return totals
        grad_left, grad_right, grad_rel = lax.map(holder, jnp.arange(N_DOM, dtype=jnp.int32))
        rel_total = rel_total + lax.optimization_barrier(jnp.sum(grad_rel, axis=0))
        grad_right = jnp.roll(grad_right, shift_by, axis=0)
        left_emb, left_state = adagrad(left_emb, left_state, grad_left.reshape(ENTS, D))
        right_emb, right_state = adagrad(right_emb, right_state, grad_right.reshape(ENTS, D))
    relation_grad = rel_total * (ROUNDS * EDGES) ** (-0.5)
    return (left_emb, left_state, right_emb, right_state, relation_grad)
```

```python
import functools

import jax
import jax.numpy as jnp
from jax import lax
from jax.experimental import pallas as pl
from jax.experimental.pallas import tpu as pltpu
from jax.sharding import PartitionSpec as P

ROUNDS = 2
STEP_SIZE = 0.1
EPSILON = 1e-10
MESH = pl.DeviceIdType.MESH
F32 = jnp.float32
BF16 = jnp.bfloat16
NT = (((1,), (1,)), ((), ()))
NN = (((1,), (0,)), ((), ()))
SEMS = 112


def dot(a, b, dims=NN):
    return lax.dot_general(a, b, dims, preferred_element_type=F32)


def split2(value):
    high = value.astype(BF16)
    return high, (value - high.astype(F32)).astype(BF16)


def window_kernel(
    dom_size, rel_scale,
    left_ref, left_state_ref, right_ref, right_state_ref, rel_ref, src_ref, relid_ref, dst_ref, neg_ref,
    left_out, left_state_out, right_out, right_state_out, rel_out,
    left_t, right_t, left_s, right_s, tab_l, tab_r, src_pos, right_pos,
    rel_rows, left_rows, anchor, right_rows, right_tr, weights, src_hl, right_hl,
    core_send, core_recv, x_send_r, x_recv_r, z_send_r, z_recv_r, own_r,
    x_send_l, x_recv_l, z_send_l, z_recv_l, y_send, y_recv,
    rel_part, rel_recv, send_sem, recv_sem,
):
    width, rows = left_t.shape
    edges = src_ref.shape[1]
    negs = neg_ref.shape[1]
    rels = rel_ref.shape[0]
    n_right = edges + negs
    neg_count = edges - 1 + negs
    dom = lax.axis_index("dom")
    row = lax.axis_index("row")
    x, z, c = row // 4, (row // 2) % 2, row % 2

    def row_peer(dx, dz, dc):
        return ((x + dx) % 4) * 4 + ((z + dz) % 2) * 2 + (c + dc) % 2

    core_peer = (dom, row_peer(0, 0, 1))
    z_peer = (dom, row_peer(0, 1, 0))
    x_peers = {dx: (dom, row_peer(dx, 0, 0)) for dx in (1, 2, 3)}
    y_peer = ((dom + dom_size // 2) % dom_size, row)
    if dom_size == 16:
        dom_groups = [
            {j: ((dom + 4 * j) % 16, row) for j in (1, 2, 3)},
            {j: ((dom // 4) * 4 + (dom % 4 + j) % 4, row) for j in (1, 2, 3)},
        ]
    else:
        dom_groups = [{2: y_peer}]
    peers = [core_peer, z_peer, *x_peers.values()]
    for group in dom_groups:
        peers += list(group.values())

    barrier = pltpu.get_barrier_semaphore()
    for peer in peers:
        pl.semaphore_signal(barrier, inc=1, device_id=peer, device_id_type=MESH)

    copies = []

    def send(src, dst, peer):
        k = len(copies)
        copy = pltpu.make_async_remote_copy(
            src_ref=src, dst_ref=dst, send_sem=send_sem.at[k], recv_sem=recv_sem.at[k],
            device_id=peer, device_id_type=MESH,
        )
        copy.start()
        copies.append(copy)
        return copy

    def place(cx, xx, zz):
        return cx * 8 + xx * 2 + zz

    mine = place(c, x, z)

    def positions(ids):
        return ((ids // 128) % 2) * 1024 + (ids // 256) * 128 + ids % 128

    def gather_left_start(rd):
        tab = tab_l.at[rd]
        own = tab.at[mine]
        zc = send(own, own, z_peer)
        xc = {dx: send(own, own, x_peers[dx]) for dx in (2, 1, 3)}
        return zc, xc

    def gather_right_start(rd):
        own = tab_r.at[rd, mine]
        xc = {dx: send(own, own, x_peers[dx]) for dx in (2, 1, 3)}
        zc = {0: send(own, own, z_peer)}
        return xc, zc

    def core_pair(tab, xx):
        part = tab.at[pl.ds(c * 8 + xx * 2, 2)]
        return send(part, part, core_peer)

    def gather_left_forward(rd, state):
        tab = tab_l.at[rd]
        zc, xc = state
        zc.wait_recv()
        other = tab.at[place(c, x, 1 - z)]
        xc2 = {dx: send(other, other, x_peers[dx]) for dx in (2, 1, 3)}
        return xc, xc2, [core_pair(tab, x)]

    def gather_left_core(rd, state):
        xc, xc2, cores = state
        for dx in (1, 3, 2):
            xc[dx].wait_recv()
            xc2[dx].wait_recv()
            cores.append(core_pair(tab_l.at[rd], (x + 4 - dx) % 4))
        return cores

    def gather_right_forward(rd, state):
        xc, zc = state
        tab = tab_r.at[rd]
        for dx in (1, 3, 2):
            xc[dx].wait_recv()
            got = tab.at[place(c, (x + 4 - dx) % 4, z)]
            zc[dx] = send(got, got, z_peer)
        return zc

    def gather_right_core(rd, zc):
        cores = []
        for dx in (0, 1, 3, 2):
            zc[dx].wait_recv()
            cores.append(core_pair(tab_r.at[rd], (x + 4 - dx) % 4))
        return cores

    def pick(tab, ids_ref, out_ref, tile_start, tile_len):
        table = jnp.concatenate([tab[p] for p in range(16)], axis=1)
        ids = ids_ref[:, pl.ds(tile_start, tile_len)]
        hot = lax.broadcasted_iota(jnp.int32, (16 * rows, tile_len), 0) == ids
        out_ref[:, pl.ds(tile_start, tile_len)] = dot(table, hot.astype(F32).astype(BF16)).astype(BF16)

    def scatter_unit(hl_ref, ids_ref, core, xx):
        sub = lax.broadcasted_iota(jnp.int32, (2 * rows, 1), 0)
        base = core * 8 * rows + xx * 2 * rows
        target = base + jnp.where(sub < rows, sub + (1 - z) * rows, sub - rows + z * rows)
        hot = (target == ids_ref[...]).astype(F32).astype(BF16)
        both = dot(hl_ref[...], hot, NT)
        return both[:width] + both[width:]

    def adagrad(rows_ref, state_ref, grad):
        state = state_ref[...] + jnp.sum(grad * grad, axis=0, keepdims=True) * (1.0 / width)
        state_ref[...] = state
        new = rows_ref[...] - grad * (STEP_SIZE / (jnp.sqrt(state) + EPSILON))
        rows_ref[...] = new
        return new

    left_t[...] = left_ref[...].T
    right_t[...] = right_ref[...].T
    tab_l[0, mine] = left_t[...].astype(BF16)
    tab_r[0, mine] = right_t[...].astype(BF16)
    left_s[...] = left_state_ref[...]
    right_s[...] = right_state_ref[...]
    pl.semaphore_wait(barrier, len(peers))

    left_state = gather_left_start(0)
    right_state = gather_right_start(0)

    rel_total = None
    for rd in range(ROUNDS):
        src_pos[...] = positions(src_ref[rd : rd + 1, :])
        right_pos[:, :edges] = positions(dst_ref[rd : rd + 1, :])
        right_pos[:, edges:] = positions(neg_ref[rd : rd + 1, :])
        rel_hot = (
            lax.broadcasted_iota(jnp.int32, (rels, edges), 0) == relid_ref[rd : rd + 1, :]
        ).astype(F32)
        rel_hot = rel_hot.astype(BF16)
        rel_value = rel_ref[...]
        high = rel_value.astype(BF16)
        rest = rel_value - high.astype(F32)
        mid = rest.astype(BF16)
        low = (rest - mid.astype(F32)).astype(BF16)
        rel_parts = jnp.concatenate([high.astype(F32).T, mid.astype(F32).T, low.astype(F32).T], axis=1)
        rel_rows[...] = dot(rel_parts.astype(BF16), jnp.concatenate([rel_hot] * 3, axis=0))

        left_state = gather_left_forward(rd, left_state)
        right_z = gather_right_forward(rd, right_state)
        left_cores = gather_left_core(rd, left_state)
        for copy in left_cores:
            copy.wait_recv()

        def pick_left(t, carry):
            pick(tab_l.at[rd], src_pos, left_rows, pl.multiple_of(t * 256, 256), 256)
            return carry

        lax.fori_loop(0, edges // 256, pick_left, 0)
        anchor[...] = (left_rows[...].astype(F32) * rel_rows[...]).astype(BF16)

        right_cores = gather_right_core(rd, right_z)
        for copy in right_cores:
            copy.wait_recv()

        def pick_right(t, carry):
            pick(tab_r.at[rd], right_pos, right_rows, pl.multiple_of(t * 256, 256), 256)
            return carry

        lax.fori_loop(0, edges // 256, pick_right, 0)
        pick(tab_r.at[rd], right_pos, right_rows, edges, negs)
        right_tr[...] = right_rows[...].astype(F32).T.astype(BF16)

        def score_block(b, carry):
            at = pl.multiple_of(b * 128, 128)
            scores = dot(right_tr[pl.ds(at, 128), :], anchor[...])
            weights[pl.ds(at, 128), :] = ((1.0 / (1.0 + jnp.exp(-scores))) * (1.0 / neg_count)).astype(BF16)
            return carry

        lax.fori_loop(0, n_right // 128, score_block, 0)

        def diag_block(b, carry):
            at = pl.multiple_of(b * 128, 128)
            scores = dot(right_tr[pl.ds(at, 128), :], anchor[:, pl.ds(at, 128)])
            eye = lax.broadcasted_iota(jnp.int32, (128, 128), 0) == lax.broadcasted_iota(jnp.int32, (128, 128), 1)
            own = -1.0 / (1.0 + jnp.exp(scores))
            rest = weights[pl.ds(at, 128), pl.ds(at, 128)].astype(F32)
            weights[pl.ds(at, 128), pl.ds(at, 128)] = jnp.where(eye, own, rest).astype(BF16)
            return carry

        lax.fori_loop(0, edges // 128, diag_block, 0)

        def grad_right(at, size):
            g = dot(anchor[...], weights[pl.ds(at, size), :], NT)
            high, low = split2(g)
            right_hl[:width, pl.ds(at, size)] = high
            right_hl[width:, pl.ds(at, size)] = low

        def grad_right_loop(t, carry):
            grad_right(pl.multiple_of(t * 256, 256), 256)
            return carry

        lax.fori_loop(0, edges // 256, grad_right_loop, 0)
        grad_right(edges, negs)

        order = (2, 1, 3, 0)

        def core_phase(hl_ref, ids_ref, base):
            sent = []
            for k, dx in enumerate(order):
                core_send[base + k] = scatter_unit(hl_ref, ids_ref, 1 - c, (x + dx) % 4)
                sent.append(send(core_send.at[base + k], core_recv.at[base + k], core_peer))
            return sent

        base = rd * 8
        sent = core_phase(right_hl, right_pos, base)
        z_copies = []
        for k, dx in enumerate(order):
            unit = scatter_unit(right_hl, right_pos, c, (x + dx) % 4)
            sent[k].wait_recv()
            unit = unit + core_recv[base + k]
            z_send_r[rd, k] = unit[:, :rows].astype(BF16)
            z_copies.append(send(z_send_r.at[rd, k], z_recv_r.at[rd, k], z_peer))
            own_r[k] = unit[:, rows:]

        def grad_left_loop(t, acc):
            at = pl.multiple_of(t * 256, 256)
            tile = pl.ds(at, 256)
            g = dot(right_rows[...], weights[:, tile])
            high, low = split2(g * rel_rows[:, tile])
            src_hl[:width, tile] = high
            src_hl[width:, tile] = low
            high, low = split2(g * left_rows[:, tile].astype(F32))
            hot = (
                lax.broadcasted_iota(jnp.int32, (128, 256), 0) == relid_ref[rd : rd + 1, tile]
            ).astype(F32)
            hot = hot.astype(BF16)
            return acc + dot(high, hot, NT) + dot(low, hot, NT)

        rel_acc = lax.fori_loop(0, edges // 256, grad_left_loop, jnp.zeros((width, 128), F32))
        rel_term = rel_acc.T[:rels]
        rel_total = rel_term if rel_total is None else rel_total + rel_term

        base = rd * 8 + 4
        sent = core_phase(src_hl, src_pos, base)
        x_copies = []
        own_l = None
        for k, dx in enumerate(order):
            unit = scatter_unit(src_hl, src_pos, c, (x + dx) % 4)
            sent[k].wait_recv()
            unit = unit + core_recv[base + k]
            if dx:
                x_send_l[rd, k] = unit.astype(BF16)
                x_copies.append(send(x_send_l.at[rd, k], x_recv_l.at[rd, k], x_peers[dx]))
            else:
                own_l = unit

        rel_stages = []
        if rd == ROUNDS - 1:
            rel_part[0] = rel_total
            rel_stages.append(send(rel_part.at[0], rel_recv.at[0], core_peer))

        right_x = []
        for k, dx in enumerate(order):
            z_copies[k].wait_recv()
            total = own_r[k] + z_recv_r[rd, k].astype(F32)
            if dx:
                x_send_r[rd, k] = total.astype(BF16)
                right_x.append(send(x_send_r.at[rd, k], x_recv_r.at[rd, k], x_peers[dx]))
            else:
                right_own = total
        own_r[3] = right_own

        def rel_step(slot, copies_in, last):
            values = {}
            for j, (copy, at) in copies_in.items():
                copy.wait_recv()
                values[j] = rel_recv[at]
            own = rel_part[slot]
            if len(values) == 3:
                total = (own + values[2]) + (values[1] + values[3])
            else:
                (only,) = values.values()
                total = own + only
            rel_part[slot + 1] = total
            return total

        if rd == ROUNDS - 1:
            rel_step(0, {0: (rel_stages[0], 0)}, False)
            rel_x = {j: (send(rel_part.at[1], rel_recv.at[j], x_peers[j]), j) for j in (1, 2, 3)}

        total = own_l
        for k in range(3):
            x_copies[k].wait_recv()
            total = total + x_recv_l[rd, k].astype(F32)
        z_send_l[rd] = total[:, :rows].astype(BF16)
        left_z = send(z_send_l.at[rd], z_recv_l.at[rd], z_peer)
        left_own = total[:, rows:]

        if rd == ROUNDS - 1:
            rel_step(1, rel_x, False)
            rel_z = {0: (send(rel_part.at[2], rel_recv.at[4], z_peer), 4)}

        total = own_r[3]
        for k in range(3):
            right_x[k].wait_recv()
            total = total + x_recv_r[rd, k].astype(F32)

        if rd < ROUNDS - 1:
            new = adagrad(right_t, right_s, total)
            y_send[...] = new.astype(BF16)
            to_holder = send(y_send, tab_r.at[rd + 1, mine], y_peer)
            left_z.wait_recv()
            new = adagrad(left_t, left_s, left_own + z_recv_l[rd].astype(F32))
            tab_l[rd + 1, mine] = new.astype(BF16)
            left_state = gather_left_start(rd + 1)
            to_holder.wait_recv()
            right_state = gather_right_start(rd + 1)
        else:
            own_r[0] = total
            to_owner = send(own_r.at[0], y_recv, y_peer)
            rel_step(2, rel_z, False)
            at = 5
            slot = 3
            rel_dom = {}
            for j, peer in dom_groups[0].items():
                rel_dom[j] = (send(rel_part.at[slot], rel_recv.at[at], peer), at)
                at += 1
            left_z.wait_recv()
            new = adagrad(left_t, left_s, left_own + z_recv_l[rd].astype(F32))
            left_out[...] = new.T
            left_state_out[...] = left_s[...]
            final = rel_step(slot, rel_dom, False)
            for group in dom_groups[1:]:
                slot += 1
                rel_dom = {}
                for j, peer in group.items():
                    rel_dom[j] = (send(rel_part.at[slot], rel_recv.at[at], peer), at)
                    at += 1
            to_owner.wait_recv()
            new = adagrad(right_t, right_s, y_recv[...])
            right_out[...] = new.T
            right_state_out[...] = right_s[...]
            if len(dom_groups) > 1:
                final = rel_step(slot, rel_dom, False)
            rel_out[...] = final * rel_scale

    for copy in copies:
        copy.wait_send()


def per_device(
    left_emb, left_state, right_emb, right_state, rel_diag, edge_src, edge_rel, edge_dst, neg_rows
):
    rows, width = left_emb.shape
    edges = edge_src.shape[1]
    negs = neg_rows.shape[2]
    rels = rel_diag.shape[0]
    n_right = edges + negs
    dom_size = lax.axis_size("dom")
    device_count = dom_size * lax.axis_size("row")
    rel_scale = (ROUNDS * edges * device_count) ** (-0.5)
    vmem = pltpu.VMEM
    outs = pl.pallas_call(
        functools.partial(window_kernel, dom_size, rel_scale),
        out_shape=(
            jax.ShapeDtypeStruct((rows, width), F32),
            jax.ShapeDtypeStruct((1, rows), F32),
            jax.ShapeDtypeStruct((rows, width), F32),
            jax.ShapeDtypeStruct((1, rows), F32),
            jax.ShapeDtypeStruct((rels, width), F32),
        ),
        in_specs=[pl.BlockSpec(memory_space=vmem)] * 9,
        out_specs=tuple([pl.BlockSpec(memory_space=vmem)] * 5),
        scratch_shapes=[
            vmem((width, rows), F32),
            vmem((width, rows), F32),
            vmem((1, rows), F32),
            vmem((1, rows), F32),
            vmem((ROUNDS, 16, width, rows), BF16),
            vmem((ROUNDS, 16, width, rows), BF16),
            vmem((1, edges), jnp.int32),
            vmem((1, n_right), jnp.int32),
            vmem((width, edges), F32),
            vmem((width, edges), BF16),
            vmem((width, edges), BF16),
            vmem((width, n_right), BF16),
            vmem((n_right, width), BF16),
            vmem((n_right, edges), BF16),
            vmem((2 * width, edges), BF16),
            vmem((2 * width, n_right), BF16),
            vmem((ROUNDS * 8, width, 2 * rows), F32),
            vmem((ROUNDS * 8, width, 2 * rows), F32),
            vmem((ROUNDS, 3, width, rows), BF16),
            vmem((ROUNDS, 3, width, rows), BF16),
            vmem((ROUNDS, 4, width, rows), BF16),
            vmem((ROUNDS, 4, width, rows), BF16),
            vmem((4, width, rows), F32),
            vmem((ROUNDS, 3, width, 2 * rows), BF16),
            vmem((ROUNDS, 3, width, 2 * rows), BF16),
            vmem((ROUNDS, width, rows), BF16),
            vmem((ROUNDS, width, rows), BF16),
            vmem((width, rows), BF16),
            vmem((width, rows), F32),
            vmem((6, rels, width), F32),
            vmem((11, rels, width), F32),
            pltpu.SemaphoreType.DMA((SEMS,)),
            pltpu.SemaphoreType.DMA((SEMS,)),
        ],
        compiler_params=pltpu.CompilerParams(
            collective_id=0, has_side_effects=True, vmem_limit_bytes=60 * 1024 * 1024
        ),
    )(
        left_emb, left_state[None], right_emb, right_state[None], rel_diag,
        edge_src, edge_rel, edge_dst, neg_rows.reshape(ROUNDS, negs),
    )
    left_new, left_sum, right_new, right_sum, rel = outs
    return left_new, left_sum.reshape(rows), right_new, right_sum.reshape(rows), rel


def solution(mesh):
    placed = (
        P(("dom", "row"), None),
        P(("dom", "row")),
        P(("dom", "row"), None),
        P(("dom", "row")),
        P(),
        P(None, ("dom", "row")),
        P(None, ("dom", "row")),
        P(None, ("dom", "row")),
        P(None, ("dom", "row"), None),
    )
    return jax.shard_map(
        per_device,
        mesh=mesh,
        in_specs=placed,
        out_specs=(
            P(("dom", "row"), None),
            P(("dom", "row")),
            P(("dom", "row"), None),
            P(("dom", "row")),
            P(),
        ),
        check_vma=False,
    )
```

```python
import functools

import jax
import jax.numpy as jnp
from jax import lax
from jax.experimental import pallas as pl
from jax.experimental.pallas import tpu as pltpu
from jax.sharding import PartitionSpec as P

ROUNDS = 2
STEP_SIZE = 0.1
EPSILON = 1e-10
MESH = pl.DeviceIdType.MESH
F32 = jnp.float32
BF16 = jnp.bfloat16
NT = (((1,), (1,)), ((), ()))
NN = (((1,), (0,)), ((), ()))
SEMS = 112


def dot(a, b, dims=NN):
    return lax.dot_general(a, b, dims, preferred_element_type=F32)


def stage(name, fn):
    with jax.named_scope(name):
        fn()


def split2(value):
    high = value.astype(BF16)
    return high, (value - high.astype(F32)).astype(BF16)


def window_kernel(
    dom_size, rel_scale,
    left_ref, left_state_ref, right_ref, right_state_ref, rel_ref, src_ref, relid_ref, dst_ref, neg_ref,
    left_out, left_state_out, right_out, right_state_out, rel_out,
    left_t, right_t, left_s, right_s, tab_l, tab_r, src_pos, right_pos,
    rel_rows, left_rows, anchor, right_rows, right_tr, weights, src_hl, right_hl,
    core_send, core_recv, x_send_r, x_recv_r, z_send_r, z_recv_r, own_r,
    x_send_l, x_recv_l, z_send_l, z_recv_l, own_l, unit_own, y_send, y_grad, y_recv,
    rel_part, rel_recv, send_sem, recv_sem,
):
    width, rows = left_t.shape
    edges = src_ref.shape[1]
    negs = neg_ref.shape[1]
    rels = rel_ref.shape[0]
    n_right = edges + negs
    neg_count = edges - 1 + negs
    dom = lax.axis_index("dom")
    row = lax.axis_index("row")
    x, z, c = row // 4, (row // 2) % 2, row % 2

    def row_peer(dx, dz, dc):
        return ((x + dx) % 4) * 4 + ((z + dz) % 2) * 2 + (c + dc) % 2

    core_peer = (dom, row_peer(0, 0, 1))
    z_peer = (dom, row_peer(0, 1, 0))
    x_peers = {dx: (dom, row_peer(dx, 0, 0)) for dx in (1, 2, 3)}
    y_peer = ((dom + dom_size // 2) % dom_size, row)
    if dom_size == 16:
        dom_groups = [
            {j: ((dom + 4 * j) % 16, row) for j in (1, 2, 3)},
            {j: ((dom // 4) * 4 + (dom % 4 + j) % 4, row) for j in (1, 2, 3)},
        ]
    else:
        dom_groups = [{2: y_peer}]
    peers = [core_peer, z_peer, *x_peers.values()]
    for group in dom_groups:
        peers += list(group.values())

    barrier = pltpu.get_barrier_semaphore()
    for peer in peers:
        pl.semaphore_signal(barrier, inc=1, device_id=peer, device_id_type=MESH)

    copies = []

    def send(src, dst, peer):
        k = len(copies)
        copy = pltpu.make_async_remote_copy(
            src_ref=src, dst_ref=dst, send_sem=send_sem.at[k], recv_sem=recv_sem.at[k],
            device_id=peer, device_id_type=MESH,
        )
        copy.start()
        copies.append(copy)
        return copy

    def place(cx, xx, zz):
        return cx * 8 + xx * 2 + zz

    mine = place(c, x, z)

    def positions(ids):
        return ((ids // 128) % 2) * 1024 + (ids // 256) * 128 + ids % 128

    def gather_left_start(rd):
        own = tab_l.at[rd, mine]
        zc = send(own, own, z_peer)
        return zc, {dx: send(own, own, x_peers[dx]) for dx in (2, 1, 3)}

    def gather_right_start(rd):
        own = tab_r.at[rd, mine]
        xc = {dx: send(own, own, x_peers[dx]) for dx in (2, 1, 3)}
        return xc, {0: send(own, own, z_peer)}

    def core_pair(tab, xx):
        part = tab.at[pl.ds(c * 8 + xx * 2, 2)]
        return send(part, part, core_peer)

    def pick_half(tab, ids_ref, out_ref, core, first):
        def tile(start, size):
            ids = ids_ref[:, pl.ds(start, size)] - core * 8 * rows
            hot = (lax.broadcasted_iota(jnp.int32, (8 * rows, size), 0) == ids).astype(F32).astype(BF16)
            table = jnp.concatenate([tab[core * 8 + p] for p in range(8)], axis=1)
            got = dot(table, hot).astype(BF16)
            if not first:
                got = got + out_ref[:, pl.ds(start, size)]
            out_ref[:, pl.ds(start, size)] = got

        def body(t, carry):
            tile(pl.multiple_of(t * 256, 256), 256)
            return carry

        count = ids_ref.shape[1]
        lax.fori_loop(0, count // 256, body, 0)
        if count % 256:
            tile(count - count % 256, count % 256)

    def pick_left(rd, core, first=False):
        stage("pick_left", lambda: pick_half(tab_l.at[rd], src_pos, left_rows, core, first))

    def pick_right(rd, core, first=False):
        stage("pick_right", lambda: pick_half(tab_r.at[rd], right_pos, right_rows, core, first))

    def scatter_unit(hl_ref, ids_ref, core, xx):
        sub = lax.broadcasted_iota(jnp.int32, (2 * rows, 1), 0)
        base = core * 8 * rows + xx * 2 * rows
        target = base + jnp.where(sub < rows, sub + (1 - z) * rows, sub - rows + z * rows)
        hot = (target == ids_ref[...]).astype(F32).astype(BF16)
        both = dot(hl_ref[...], hot, NT)
        return both[:width] + both[width:]

    def adagrad(rows_ref, state_ref, grad):
        state = state_ref[...] + jnp.sum(grad * grad, axis=0, keepdims=True) * (1.0 / width)
        state_ref[...] = state
        new = rows_ref[...] - grad * (STEP_SIZE / (jnp.sqrt(state) + EPSILON))
        rows_ref[...] = new
        return new

    def load():
        left_t[...] = left_ref[...].T
        right_t[...] = right_ref[...].T
        tab_l[0, mine] = left_t[...].astype(BF16)
        tab_r[0, mine] = right_t[...].astype(BF16)
        left_s[...] = left_state_ref[...]
        right_s[...] = right_state_ref[...]

    stage("load_transpose", load)
    pl.semaphore_wait(barrier, len(peers))

    right_state = gather_right_start(0)
    left_state = gather_left_start(0)

    rel_total = None
    for rd in range(ROUNDS):
        def indices():
            src_pos[...] = positions(src_ref[rd : rd + 1, :])
            right_pos[:, :edges] = positions(dst_ref[rd : rd + 1, :])
            right_pos[:, edges:] = positions(neg_ref[rd : rd + 1, :])
            rel_hot = (
                lax.broadcasted_iota(jnp.int32, (rels, edges), 0) == relid_ref[rd : rd + 1, :]
            ).astype(F32)
            rel_hot = rel_hot.astype(BF16)
            rel_value = rel_ref[...]
            high = rel_value.astype(BF16)
            rest = rel_value - high.astype(F32)
            mid = rest.astype(BF16)
            low = (rest - mid.astype(F32)).astype(BF16)
            rel_parts = jnp.concatenate([high.astype(F32).T, mid.astype(F32).T, low.astype(F32).T], axis=1)
            rel_rows[...] = dot(rel_parts.astype(BF16), jnp.concatenate([rel_hot] * 3, axis=0))

        stage("indices_relation", indices)

        right_x, right_z = right_state
        left_z, left_x = left_state
        left_cores, right_cores = {}, {}
        left_z.wait_recv()
        got = tab_l.at[rd, place(c, x, 1 - z)]
        left_x2 = {dx: send(got, got, x_peers[dx]) for dx in (2, 1, 3)}
        left_cores[0] = core_pair(tab_l.at[rd], x)
        for dx in (1, 3, 2):
            right_x[dx].wait_recv()
            got = tab_r.at[rd, place(c, (x + 4 - dx) % 4, z)]
            right_z[dx] = send(got, got, z_peer)
        for dx in (0, 1, 3, 2):
            from_x = (x + 4 - dx) % 4
            right_z[dx].wait_recv()
            right_cores[dx] = core_pair(tab_r.at[rd], from_x)
            if dx:
                left_x[dx].wait_recv()
                left_x2[dx].wait_recv()
                left_cores[dx] = core_pair(tab_l.at[rd], from_x)
        pick_left(rd, c, True)
        pick_right(rd, c, True)
        for dx in (0, 1, 3, 2):
            left_cores[dx].wait_recv()
        pick_left(rd, 1 - c)
        for dx in (0, 1, 3, 2):
            right_cores[dx].wait_recv()
        pick_right(rd, 1 - c)

        def transposes():
            anchor[...] = (left_rows[...].astype(F32) * rel_rows[...]).astype(BF16)
            right_tr[...] = right_rows[...].astype(F32).T.astype(BF16)

        stage("anchor_transpose", transposes)

        def score_tile(t, carry):
            tile = pl.ds(pl.multiple_of(t * 256, 256), 256)
            scores = dot(right_tr[...], anchor[:, tile])
            weights[:, tile] = ((1.0 / (1.0 + jnp.exp(-scores))) * (1.0 / neg_count)).astype(BF16)
            scores = dot(right_tr[tile, :], anchor[:, tile])
            eye = lax.broadcasted_iota(jnp.int32, (256, 256), 0) == lax.broadcasted_iota(jnp.int32, (256, 256), 1)
            own = -1.0 / (1.0 + jnp.exp(scores))
            rest = weights[tile, tile].astype(F32)
            weights[tile, tile] = jnp.where(eye, own, rest).astype(BF16)
            return carry

        stage("scores", lambda: lax.fori_loop(0, edges // 256, score_tile, 0))

        def grad_right(at, size):
            g = dot(anchor[...], weights[pl.ds(at, size), :], NT)
            high, low = split2(g)
            right_hl[:width, pl.ds(at, size)] = high
            right_hl[width:, pl.ds(at, size)] = low

        def grad_right_loop(t, carry):
            grad_right(pl.multiple_of(t * 256, 256), 256)
            return carry

        def grad_right_all():
            lax.fori_loop(0, edges // 256, grad_right_loop, 0)
            grad_right(edges, negs)

        stage("grad_right", grad_right_all)

        order = (2, 1, 3, 0)

        def scatter(name, hl_ref, ids_ref, base, use):
            sent = {}

            def partner(k):
                def part():
                    core_send[base + k] = scatter_unit(hl_ref, ids_ref, 1 - c, (x + order[k]) % 4)

                stage(name, part)
                sent[k] = send(core_send.at[base + k], core_recv.at[base + k], core_peer)

            def own(k):
                def part():
                    unit_own[...] = scatter_unit(hl_ref, ids_ref, c, (x + order[k]) % 4)

                stage(name, part)
                sent[k].wait_recv()
                use(k, unit_own[...] + core_recv[base + k])

            partner(0)
            partner(1)
            own(0)
            partner(2)
            own(1)
            partner(3)
            own(2)
            own(3)

        right_x = {}

        def use_right(k, unit):
            if order[k]:
                x_send_r[rd, k] = unit.astype(BF16)
                right_x[k] = send(x_send_r.at[rd, k], x_recv_r.at[rd, k], x_peers[order[k]])
            else:
                own_r[...] = unit

        scatter("scatter_right", right_hl, right_pos, rd * 8, use_right)

        def grad_left_loop(t, acc):
            at = pl.multiple_of(t * 256, 256)
            tile = pl.ds(at, 256)
            g = dot(right_rows[...], weights[:, tile])
            high, low = split2(g * rel_rows[:, tile])
            src_hl[:width, tile] = high
            src_hl[width:, tile] = low
            high, low = split2(g * left_rows[:, tile].astype(F32))
            hot = (
                lax.broadcasted_iota(jnp.int32, (128, 256), 0) == relid_ref[rd : rd + 1, tile]
            ).astype(F32)
            hot = hot.astype(BF16)
            return acc + dot(high, hot, NT) + dot(low, hot, NT)

        def grad_left_all():
            rel_acc = lax.fori_loop(0, edges // 256, grad_left_loop, jnp.zeros((width, 128), F32))
            rel_part[5] = rel_acc.T[:rels]

        stage("grad_left", grad_left_all)
        rel_term = rel_part[5]
        rel_total = rel_term if rel_total is None else rel_total + rel_term
        last = rd == ROUNDS - 1
        rel_wait = None

        def rel_start(slot, at, group):
            return {j: (send(rel_part.at[slot], rel_recv.at[at + n], group[j]), at + n) for n, j in enumerate(group)}

        def rel_step(slot, arriving):
            values = {}
            for j, (copy, at) in arriving.items():
                copy.wait_recv()
                values[j] = rel_recv[at]
            own = rel_part[slot]
            if len(values) == 3:
                total = (own + values[2]) + (values[1] + values[3])
            else:
                (only,) = values.values()
                total = own + only
            rel_part[slot + 1] = total

        if last:
            rel_part[0] = rel_total
            rel_wait = rel_start(0, 0, {1: core_peer})

        left_z = {}

        def use_left(k, unit):
            z_send_l[rd, k] = unit[:, :rows].astype(BF16)
            left_z[k] = send(z_send_l.at[rd, k], z_recv_l.at[rd, k], z_peer)
            own_l[k] = unit[:, rows:]

        scatter("scatter_left", src_hl, src_pos, rd * 8 + 4, use_left)

        if last:
            rel_step(0, rel_wait)
            rel_wait = rel_start(1, 1, x_peers)

        total = own_r[...]
        for k in range(3):
            right_x[k].wait_recv()
            total = total + x_recv_r[rd, k].astype(F32)
        z_send_r[rd] = total[:, :rows].astype(BF16)
        right_z = send(z_send_r.at[rd], z_recv_r.at[rd], z_peer)
        own_r[:, rows:] = total[:, rows:]

        left_x = {}

        def left_on(k):
            left_z[k].wait_recv()
            total = own_l[k] + z_recv_l[rd, k].astype(F32)
            if order[k]:
                x_send_l[rd, k] = total.astype(BF16)
                left_x[k] = send(x_send_l.at[rd, k], x_recv_l.at[rd, k], x_peers[order[k]])
            else:
                own_l[k] = total

        left_on(0)
        left_on(1)
        if last:
            rel_step(1, rel_wait)
            rel_wait = rel_start(2, 4, {1: z_peer})

        right_z.wait_recv()
        total = own_r[:, rows:] + z_recv_r[rd].astype(F32)
        if last:
            y_grad[...] = total
            to_owner = send(y_grad, y_recv, y_peer)
        else:
            new = adagrad(right_t, right_s, total)
            y_send[...] = new.astype(BF16)
            to_holder = send(y_send, tab_r.at[rd + 1, mine], y_peer)
        left_on(2)
        if last:
            rel_step(2, rel_wait)
            rel_wait = rel_start(3, 5, dom_groups[0])
        left_on(3)
        if not last:
            to_holder.wait_recv()
            right_state = gather_right_start(rd + 1)
        total = own_l[3]
        for k in range(3):
            left_x[k].wait_recv()
            total = total + x_recv_l[rd, k].astype(F32)
        new = adagrad(left_t, left_s, total)
        if not last:
            tab_l[rd + 1, mine] = new.astype(BF16)
            left_state = gather_left_start(rd + 1)
        else:
            rel_step(3, rel_wait)
            if len(dom_groups) > 1:
                rel_wait = rel_start(4, 8, dom_groups[1])
            left_out[...] = new.T
            left_state_out[...] = left_s[...]
            to_owner.wait_recv()
            new = adagrad(right_t, right_s, y_recv[...])
            right_out[...] = new.T
            right_state_out[...] = right_s[...]
            if len(dom_groups) > 1:
                rel_step(4, rel_wait)
            rel_out[...] = rel_part[3 + len(dom_groups)] * rel_scale

    for copy in copies:
        copy.wait_send()


def per_device(
    left_emb, left_state, right_emb, right_state, rel_diag, edge_src, edge_rel, edge_dst, neg_rows
):
    rows, width = left_emb.shape
    edges = edge_src.shape[1]
    negs = neg_rows.shape[2]
    rels = rel_diag.shape[0]
    n_right = edges + negs
    dom_size = lax.axis_size("dom")
    device_count = dom_size * lax.axis_size("row")
    rel_scale = (ROUNDS * edges * device_count) ** (-0.5)
    vmem = pltpu.VMEM
    outs = pl.pallas_call(
        functools.partial(window_kernel, dom_size, rel_scale),
        out_shape=(
            jax.ShapeDtypeStruct((rows, width), F32),
            jax.ShapeDtypeStruct((1, rows), F32),
            jax.ShapeDtypeStruct((rows, width), F32),
            jax.ShapeDtypeStruct((1, rows), F32),
            jax.ShapeDtypeStruct((rels, width), F32),
        ),
        in_specs=[pl.BlockSpec(memory_space=vmem)] * 9,
        out_specs=tuple([pl.BlockSpec(memory_space=vmem)] * 5),
        scratch_shapes=[
            vmem((width, rows), F32),
            vmem((width, rows), F32),
            vmem((1, rows), F32),
            vmem((1, rows), F32),
            vmem((ROUNDS, 16, width, rows), BF16),
            vmem((ROUNDS, 16, width, rows), BF16),
            vmem((1, edges), jnp.int32),
            vmem((1, n_right), jnp.int32),
            vmem((width, edges), F32),
            vmem((width, edges), BF16),
            vmem((width, edges), BF16),
            vmem((width, n_right), BF16),
            vmem((n_right, width), BF16),
            vmem((n_right, edges), BF16),
            vmem((2 * width, edges), BF16),
            vmem((2 * width, n_right), BF16),
            vmem((ROUNDS * 8, width, 2 * rows), F32),
            vmem((ROUNDS * 8, width, 2 * rows), F32),
            vmem((ROUNDS, 3, width, 2 * rows), BF16),
            vmem((ROUNDS, 3, width, 2 * rows), BF16),
            vmem((ROUNDS, width, rows), BF16),
            vmem((ROUNDS, width, rows), BF16),
            vmem((width, 2 * rows), F32),
            vmem((ROUNDS, 3, width, rows), BF16),
            vmem((ROUNDS, 3, width, rows), BF16),
            vmem((ROUNDS, 4, width, rows), BF16),
            vmem((ROUNDS, 4, width, rows), BF16),
            vmem((4, width, rows), F32),
            vmem((width, 2 * rows), F32),
            vmem((width, rows), BF16),
            vmem((width, rows), F32),
            vmem((width, rows), F32),
            vmem((6, rels, width), F32),
            vmem((11, rels, width), F32),
            pltpu.SemaphoreType.DMA((SEMS,)),
            pltpu.SemaphoreType.DMA((SEMS,)),
        ],
        compiler_params=pltpu.CompilerParams(
            collective_id=0, has_side_effects=True, vmem_limit_bytes=60 * 1024 * 1024
        ),
    )(
        left_emb, left_state[None], right_emb, right_state[None], rel_diag,
        edge_src, edge_rel, edge_dst, neg_rows.reshape(ROUNDS, negs),
    )
    left_new, left_sum, right_new, right_sum, rel = outs
    return left_new, left_sum.reshape(rows), right_new, right_sum.reshape(rows), rel


def solution(mesh):
    placed = (
        P(("dom", "row"), None),
        P(("dom", "row")),
        P(("dom", "row"), None),
        P(("dom", "row")),
        P(),
        P(None, ("dom", "row")),
        P(None, ("dom", "row")),
        P(None, ("dom", "row")),
        P(None, ("dom", "row"), None),
    )
    return jax.shard_map(
        per_device,
        mesh=mesh,
        in_specs=placed,
        out_specs=(
            P(("dom", "row"), None),
            P(("dom", "row")),
            P(("dom", "row"), None),
            P(("dom", "row")),
            P(),
        ),
        check_vma=False,
    )
```

```python
import functools

import jax
import jax.numpy as jnp
from jax import lax
from jax.experimental import pallas as pl
from jax.experimental.pallas import tpu as pltpu
from jax.sharding import PartitionSpec as P

ROUNDS = 2
STEP_SIZE = 0.1
EPSILON = 1e-10
MESH = pl.DeviceIdType.MESH
F32 = jnp.float32
BF16 = jnp.bfloat16
NT = (((1,), (1,)), ((), ()))
NN = (((1,), (0,)), ((), ()))
SEMS = 128


def dot(a, b, dims=NN):
    return lax.dot_general(a, b, dims, preferred_element_type=F32)


def stage(name, fn):
    with jax.named_scope(name):
        fn()


def split2(value):
    high = value.astype(BF16)
    return high, (value - high.astype(F32)).astype(BF16)


def window_kernel(
    dom_size, rel_scale,
    left_ref, left_state_ref, right_ref, right_state_ref, rel_ref, src_ref, relid_ref, dst_ref, neg_ref,
    left_out, left_state_out, right_out, right_state_out, rel_out,
    left_t, right_t, left_s, right_s, tab_l, tab_r, src_pos, right_pos,
    rel_rows, left_rows, anchor, right_rows, right_tr, weights, src_hl, right_hl,
    core_send, core_recv, unit_own,
    xa_send, xa_recv, za_send, za_recv, own_a, zb_send, zb_recv, xb_send, xb_recv, own_b, y_send, y_grad, y_recv,
    rel_part, rel_recv, send_sem, recv_sem,
):
    width, rows = left_t.shape
    top = width // 2 // 16 * 16
    edges = src_ref.shape[1]
    negs = neg_ref.shape[1]
    rels = rel_ref.shape[0]
    n_right = edges + negs
    neg_count = edges - 1 + negs
    dom = lax.axis_index("dom")
    row = lax.axis_index("row")
    x, z, c = row // 4, (row // 2) % 2, row % 2

    def row_peer(dx, dz, dc):
        return ((x + dx) % 4) * 4 + ((z + dz) % 2) * 2 + (c + dc) % 2

    core_peer = (dom, row_peer(0, 0, 1))
    z_peer = (dom, row_peer(0, 1, 0))
    x_peers = {dx: (dom, row_peer(dx, 0, 0)) for dx in (1, 2, 3)}
    y_peer = ((dom + dom_size // 2) % dom_size, row)
    if dom_size == 16:
        dom_groups = [
            {j: ((dom + 4 * j) % 16, row) for j in (1, 2, 3)},
            {j: ((dom // 4) * 4 + (dom % 4 + j) % 4, row) for j in (1, 2, 3)},
        ]
    else:
        dom_groups = [{2: y_peer}]
    peers = [core_peer, z_peer, *x_peers.values()]
    for group in dom_groups:
        peers += list(group.values())

    barrier = pltpu.get_barrier_semaphore()
    for peer in peers:
        pl.semaphore_signal(barrier, inc=1, device_id=peer, device_id_type=MESH)

    copies = []

    def send(src, dst, peer):
        k = len(copies)
        copy = pltpu.make_async_remote_copy(
            src_ref=src, dst_ref=dst, send_sem=send_sem.at[k], recv_sem=recv_sem.at[k],
            device_id=peer, device_id_type=MESH,
        )
        copy.start()
        copies.append(copy)
        return copy

    def place(cx, xx, zz):
        return cx * 8 + xx * 2 + zz

    mine = place(c, x, z)

    def positions(ids):
        return ((ids // 128) % 2) * 1024 + (ids // 256) * 128 + ids % 128

    def gather_left_start(rd):
        own = tab_l.at[rd, mine]
        zc = send(own, own, z_peer)
        return zc, {dx: send(own, own, x_peers[dx]) for dx in (2, 1, 3)}

    def gather_right_start(rd):
        own = tab_r.at[rd, mine]
        xc = {dx: send(own, own, x_peers[dx]) for dx in (2, 1, 3)}
        return xc, {0: send(own, own, z_peer)}

    def core_pair(tab, xx):
        part = tab.at[pl.ds(c * 8 + xx * 2, 2)]
        return send(part, part, core_peer)

    def pick_half(tab, ids_ref, out_ref, core, first):
        def tile(start, size):
            ids = ids_ref[:, pl.ds(start, size)] - core * 8 * rows
            hot = (lax.broadcasted_iota(jnp.int32, (8 * rows, size), 0) == ids).astype(F32).astype(BF16)
            table = jnp.concatenate([tab[core * 8 + p] for p in range(8)], axis=1)
            got = dot(table, hot).astype(BF16)
            if not first:
                got = got + out_ref[:, pl.ds(start, size)]
            out_ref[:, pl.ds(start, size)] = got

        def body(t, carry):
            tile(pl.multiple_of(t * 256, 256), 256)
            return carry

        count = ids_ref.shape[1]
        lax.fori_loop(0, count // 256, body, 0)
        if count % 256:
            tile(count - count % 256, count % 256)

    def pick_left(rd, core, first=False):
        stage("pick_left", lambda: pick_half(tab_l.at[rd], src_pos, left_rows, core, first))

    def pick_right(rd, core, first=False):
        stage("pick_right", lambda: pick_half(tab_r.at[rd], right_pos, right_rows, core, first))

    def scatter_unit(hl_ref, ids_ref, core, xx):
        sub = lax.broadcasted_iota(jnp.int32, (2 * rows, 1), 0)
        base = core * 8 * rows + xx * 2 * rows
        target = base + jnp.where(sub < rows, sub + (1 - z) * rows, sub - rows + z * rows)
        hot = (target == ids_ref[...]).astype(F32).astype(BF16)
        both = dot(hl_ref[...], hot, NT)
        return both[:width] + both[width:]

    def adagrad(rows_ref, state_ref, grad):
        state = state_ref[...] + jnp.sum(grad * grad, axis=0, keepdims=True) * (1.0 / width)
        state_ref[...] = state
        new = rows_ref[...] - grad * (STEP_SIZE / (jnp.sqrt(state) + EPSILON))
        rows_ref[...] = new
        return new

    def load():
        left_t[...] = left_ref[...]
        right_t[...] = right_ref[...]
        tab_l[0, mine] = left_t[...].astype(BF16)
        tab_r[0, mine] = right_t[...].astype(BF16)
        left_s[...] = left_state_ref[...]
        right_s[...] = right_state_ref[...]

    stage("load_transpose", load)
    pl.semaphore_wait(barrier, len(peers))

    right_state = gather_right_start(0)
    left_state = gather_left_start(0)

    rel_total = None
    for rd in range(ROUNDS):
        def indices():
            src_pos[...] = positions(src_ref[rd : rd + 1, :])
            right_pos[:, :edges] = positions(dst_ref[rd : rd + 1, :])
            right_pos[:, edges:] = positions(neg_ref[rd : rd + 1, :])
            rel_hot = (
                lax.broadcasted_iota(jnp.int32, (rels, edges), 0) == relid_ref[rd : rd + 1, :]
            ).astype(F32)
            rel_hot = rel_hot.astype(BF16)
            rel_value = rel_ref[...]
            high = rel_value.astype(BF16)
            rest = rel_value - high.astype(F32)
            mid = rest.astype(BF16)
            low = (rest - mid.astype(F32)).astype(BF16)
            rel_parts = jnp.concatenate([high.astype(F32).T, mid.astype(F32).T, low.astype(F32).T], axis=1)
            rel_rows[...] = dot(rel_parts.astype(BF16), jnp.concatenate([rel_hot] * 3, axis=0))

        stage("indices_relation", indices)

        right_x, right_z = right_state
        left_z, left_x = left_state
        left_cores, right_cores = {}, {}
        left_z.wait_recv()
        got = tab_l.at[rd, place(c, x, 1 - z)]
        left_x2 = {dx: send(got, got, x_peers[dx]) for dx in (2, 1, 3)}
        left_cores[0] = core_pair(tab_l.at[rd], x)
        for dx in (1, 3, 2):
            right_x[dx].wait_recv()
            got = tab_r.at[rd, place(c, (x + 4 - dx) % 4, z)]
            right_z[dx] = send(got, got, z_peer)
        for dx in (0, 1, 3, 2):
            right_z[dx].wait_recv()
            right_cores[dx] = core_pair(tab_r.at[rd], (x + 4 - dx) % 4)
        pick_right(rd, c, True)
        for dx in (1, 3, 2):
            left_x[dx].wait_recv()
            left_x2[dx].wait_recv()
            left_cores[dx] = core_pair(tab_l.at[rd], (x + 4 - dx) % 4)
        for dx in (0, 1, 3, 2):
            right_cores[dx].wait_recv()
        pick_right(rd, 1 - c)

        def transpose():
            right_tr[...] = right_rows[...].astype(F32).T.astype(BF16)

        stage("transpose", transpose)
        pick_left(rd, c, True)
        for dx in (0, 1, 3, 2):
            left_cores[dx].wait_recv()
        pick_left(rd, 1 - c)

        def anchors():
            anchor[...] = (left_rows[...].astype(F32) * rel_rows[...]).astype(BF16)

        stage("anchor", anchors)

        def score_tile(t, carry):
            tile = pl.ds(pl.multiple_of(t * 256, 256), 256)
            scores = dot(right_tr[...], anchor[:, tile])
            weights[:, tile] = ((1.0 / (1.0 + jnp.exp(-scores))) * (1.0 / neg_count)).astype(BF16)
            scores = dot(right_tr[tile, :], anchor[:, tile])
            eye = lax.broadcasted_iota(jnp.int32, (256, 256), 0) == lax.broadcasted_iota(jnp.int32, (256, 256), 1)
            own = -1.0 / (1.0 + jnp.exp(scores))
            rest = weights[tile, tile].astype(F32)
            weights[tile, tile] = jnp.where(eye, own, rest).astype(BF16)
            return carry

        stage("scores", lambda: lax.fori_loop(0, edges // 256, score_tile, 0))

        def grad_right(at, size):
            g = dot(anchor[...], weights[pl.ds(at, size), :], NT)
            high, low = split2(g)
            right_hl[:width, pl.ds(at, size)] = high
            right_hl[width:, pl.ds(at, size)] = low

        def grad_right_loop(t, carry):
            grad_right(pl.multiple_of(t * 256, 256), 256)
            return carry

        def grad_right_all():
            lax.fori_loop(0, edges // 256, grad_right_loop, 0)
            grad_right(edges, negs)

        stage("grad_right", grad_right_all)

        order = (2, 1, 3, 0)

        def scatter(name, hl_ref, ids_ref, base, use, between=lambda k: None):
            sent = {}

            def partner(k):
                def part():
                    core_send[base + k] = scatter_unit(hl_ref, ids_ref, 1 - c, (x + order[k]) % 4)

                stage(name, part)
                sent[k] = send(core_send.at[base + k], core_recv.at[base + k], core_peer)

            def own(k):
                def part():
                    unit_own[...] = scatter_unit(hl_ref, ids_ref, c, (x + order[k]) % 4)

                stage(name, part)
                sent[k].wait_recv()
                use(k, unit_own[...] + core_recv[base + k])
                between(k)

            partner(0)
            partner(1)
            own(0)
            partner(2)
            own(1)
            partner(3)
            own(2)
            own(3)

        def sums(side):
            at = rd * 2 + side
            az, ax, bx = {}, {}, {}
            part = {}

            def use(k, unit):
                if order[k]:
                    xa_send[at, k] = unit[:top].astype(BF16)
                    ax[k] = send(xa_send.at[at, k], xa_recv.at[at, k], x_peers[order[k]])
                else:
                    own_a[side] = unit[:top]
                zb_send[at, k] = unit[top:, :rows].astype(BF16)
                az[k] = send(zb_send.at[at, k], zb_recv.at[at, k], z_peer)
                own_b[side * 4 + k] = unit[top:, rows:]

            def rest_on(k):
                az[k].wait_recv()
                total = own_b[side * 4 + k] + zb_recv[at, k].astype(F32)
                if order[k]:
                    xb_send[at, k] = total.astype(BF16)
                    bx[k] = send(xb_send.at[at, k], xb_recv.at[at, k], x_peers[order[k]])
                else:
                    own_b[side * 4 + k] = total

            def top_on():
                total = own_a[side]
                for k in range(3):
                    ax[k].wait_recv()
                    total = total + xa_recv[at, k].astype(F32)
                za_send[at] = total[:, :rows].astype(BF16)
                part["z"] = send(za_send.at[at], za_recv.at[at], z_peer)
                own_a[side, :, rows:] = total[:, rows:]

            def finish():
                total = own_b[side * 4 + 3]
                for k in range(3):
                    bx[k].wait_recv()
                    total = total + xb_recv[at, k].astype(F32)
                part["z"].wait_recv()
                return jnp.concatenate([own_a[side, :, rows:] + za_recv[at].astype(F32), total], axis=0)

            return use, rest_on, top_on, finish

        right_use, right_on, right_top, right_finish = sums(0)
        left_use, left_on, left_top, left_finish = sums(1)
        scatter("scatter_right", right_hl, right_pos, rd * 8, right_use)

        def grad_left_loop(t, acc):
            at = pl.multiple_of(t * 256, 256)
            tile = pl.ds(at, 256)
            g = dot(right_rows[...], weights[:, tile])
            high, low = split2(g * rel_rows[:, tile])
            src_hl[:width, tile] = high
            src_hl[width:, tile] = low
            high, low = split2(g * left_rows[:, tile].astype(F32))
            hot = (
                lax.broadcasted_iota(jnp.int32, (128, 256), 0) == relid_ref[rd : rd + 1, tile]
            ).astype(F32)
            hot = hot.astype(BF16)
            return acc + dot(high, hot, NT) + dot(low, hot, NT)

        def grad_left_all():
            rel_acc = lax.fori_loop(0, edges // 256, grad_left_loop, jnp.zeros((width, 128), F32))
            rel_part[5] = rel_acc.T[:rels]

        stage("grad_left", grad_left_all)
        rel_term = rel_part[5]
        rel_total = rel_term if rel_total is None else rel_total + rel_term
        last = rd == ROUNDS - 1
        rel_wait = None

        def rel_start(slot, at, group):
            return {j: (send(rel_part.at[slot], rel_recv.at[at + n], group[j]), at + n) for n, j in enumerate(group)}

        def rel_step(slot, arriving):
            values = {}
            for j, (copy, at) in arriving.items():
                copy.wait_recv()
                values[j] = rel_recv[at]
            own = rel_part[slot]
            if len(values) == 3:
                total = (own + values[2]) + (values[1] + values[3])
            else:
                (only,) = values.values()
                total = own + only
            rel_part[slot + 1] = total

        if last:
            rel_part[0] = rel_total
            rel_wait = rel_start(0, 0, {1: core_peer})

        right_on(0)
        right_on(1)

        def between(k):
            nonlocal rel_wait
            if k == 0:
                right_on(2)
                right_on(3)
                if last:
                    rel_step(0, rel_wait)
                    rel_wait = rel_start(1, 1, x_peers)
            if k == 1:
                right_top()

        scatter("scatter_left", src_hl, src_pos, rd * 8 + 4, left_use, between)

        if last:
            rel_step(1, rel_wait)
            rel_wait = rel_start(2, 4, {1: z_peer})
        left_on(0)
        left_on(1)
        total = right_finish()
        if last:
            y_grad[...] = total
            to_owner = send(y_grad, y_recv, y_peer)
            rel_step(2, rel_wait)
            rel_wait = rel_start(3, 5, dom_groups[0])
        else:
            new = adagrad(right_t, right_s, total)
            y_send[...] = new.astype(BF16)
            to_holder = send(y_send, tab_r.at[rd + 1, mine], y_peer)
        left_on(2)
        left_on(3)
        left_top()
        if last:
            rel_step(3, rel_wait)
            if len(dom_groups) > 1:
                rel_wait = rel_start(4, 8, dom_groups[1])
        else:
            to_holder.wait_recv()
            right_state = gather_right_start(rd + 1)
        new = adagrad(left_t, left_s, left_finish())
        if not last:
            tab_l[rd + 1, mine] = new.astype(BF16)
            left_state = gather_left_start(rd + 1)
        else:
            left_out[...] = new
            left_state_out[...] = left_s[...]
            to_owner.wait_recv()
            new = adagrad(right_t, right_s, y_recv[...])
            right_out[...] = new
            right_state_out[...] = right_s[...]
            if len(dom_groups) > 1:
                rel_step(4, rel_wait)
            rel_out[...] = rel_part[3 + len(dom_groups)] * rel_scale

    for copy in copies:
        copy.wait_send()


def hand_out(*refs):
    for source, target in zip(refs[:5], refs[5:]):
        target[...] = source[...]


def per_device(
    left_emb, left_state, right_emb, right_state, rel_diag, edge_src, edge_rel, edge_dst, neg_rows
):
    rows, width = left_emb.shape
    edges = edge_src.shape[1]
    negs = neg_rows.shape[2]
    rels = rel_diag.shape[0]
    n_right = edges + negs
    dom_size = lax.axis_size("dom")
    device_count = dom_size * lax.axis_size("row")
    rel_scale = (ROUNDS * edges * device_count) ** (-0.5)
    vmem = pltpu.VMEM
    top = width // 2 // 16 * 16
    shapes = (
        jax.ShapeDtypeStruct((width, rows), F32),
        jax.ShapeDtypeStruct((1, rows), F32),
        jax.ShapeDtypeStruct((width, rows), F32),
        jax.ShapeDtypeStruct((1, rows), F32),
        jax.ShapeDtypeStruct((rels, width), F32),
    )
    outs = pl.pallas_call(
        functools.partial(window_kernel, dom_size, rel_scale),
        out_shape=shapes,
        in_specs=[pl.BlockSpec(memory_space=vmem)] * 9,
        out_specs=tuple([pl.BlockSpec(memory_space=vmem)] * 5),
        scratch_shapes=[
            vmem((width, rows), F32),
            vmem((width, rows), F32),
            vmem((1, rows), F32),
            vmem((1, rows), F32),
            vmem((ROUNDS, 16, width, rows), BF16),
            vmem((ROUNDS, 16, width, rows), BF16),
            vmem((1, edges), jnp.int32),
            vmem((1, n_right), jnp.int32),
            vmem((width, edges), F32),
            vmem((width, edges), BF16),
            vmem((width, edges), BF16),
            vmem((width, n_right), BF16),
            vmem((n_right, width), BF16),
            vmem((n_right, edges), BF16),
            vmem((2 * width, edges), BF16),
            vmem((2 * width, n_right), BF16),
            vmem((ROUNDS * 8, width, 2 * rows), F32),
            vmem((ROUNDS * 8, width, 2 * rows), F32),
            vmem((width, 2 * rows), F32),
            vmem((ROUNDS * 2, 3, top, 2 * rows), BF16),
            vmem((ROUNDS * 2, 3, top, 2 * rows), BF16),
            vmem((ROUNDS * 2, top, rows), BF16),
            vmem((ROUNDS * 2, top, rows), BF16),
            vmem((2, top, 2 * rows), F32),
            vmem((ROUNDS * 2, 4, width - top, rows), BF16),
            vmem((ROUNDS * 2, 4, width - top, rows), BF16),
            vmem((ROUNDS * 2, 3, width - top, rows), BF16),
            vmem((ROUNDS * 2, 3, width - top, rows), BF16),
            vmem((8, width - top, rows), F32),
            vmem((width, rows), BF16),
            vmem((width, rows), F32),
            vmem((width, rows), F32),
            vmem((6, rels, width), F32),
            vmem((11, rels, width), F32),
            pltpu.SemaphoreType.DMA((SEMS,)),
            pltpu.SemaphoreType.DMA((SEMS,)),
        ],
        compiler_params=pltpu.CompilerParams(
            collective_id=0, has_side_effects=True, vmem_limit_bytes=60 * 1024 * 1024
        ),
    )(
        left_emb.T, left_state[None], right_emb.T, right_state[None], rel_diag,
        edge_src, edge_rel, edge_dst, neg_rows.reshape(ROUNDS, negs),
    )
    left_new, left_sum, right_new, right_sum, rel = pl.pallas_call(
        hand_out,
        out_shape=shapes,
        in_specs=[pl.BlockSpec(memory_space=vmem)] * 5,
        out_specs=tuple([pl.BlockSpec(memory_space=vmem)] * 5),
    )(*outs)
    return left_new.T, left_sum.reshape(rows), right_new.T, right_sum.reshape(rows), rel


def solution(mesh):
    placed = (
        P(("dom", "row"), None),
        P(("dom", "row")),
        P(("dom", "row"), None),
        P(("dom", "row")),
        P(),
        P(None, ("dom", "row")),
        P(None, ("dom", "row")),
        P(None, ("dom", "row")),
        P(None, ("dom", "row"), None),
    )
    return jax.shard_map(
        per_device,
        mesh=mesh,
        in_specs=placed,
        out_specs=(
            P(("dom", "row"), None),
            P(("dom", "row")),
            P(("dom", "row"), None),
            P(("dom", "row")),
            P(),
        ),
        check_vma=False,
    )
```

```python
import functools

import jax
import jax.numpy as jnp
from jax import lax
from jax.experimental import pallas as pl
from jax.experimental.pallas import tpu as pltpu
from jax.sharding import PartitionSpec as P

ROUNDS = 2
STEP_SIZE = 0.1
EPSILON = 1e-10
MESH = pl.DeviceIdType.MESH
F32 = jnp.float32
BF16 = jnp.bfloat16
NT = (((1,), (1,)), ((), ()))
NN = (((1,), (0,)), ((), ()))
SEMS = 128


def dot(a, b, dims=NN):
    return lax.dot_general(a, b, dims, preferred_element_type=F32)


def stage(name, fn):
    with jax.named_scope(name):
        fn()


def split2(value):
    high = value.astype(BF16)
    return high, (value - high.astype(F32)).astype(BF16)


def window_kernel(
    dom_size, rel_scale,
    left_ref, left_state_ref, right_ref, right_state_ref, rel_ref, src_ref, relid_ref, dst_ref, neg_ref,
    left_out, left_state_out, right_out, right_state_out, rel_out,
    left_t, right_t, left_s, right_s, tab_l, tab_r, src_pos, right_pos,
    rel_rows, left_rows, anchor, right_rows, right_tr, weights, src_hl, right_hl, rel_hl,
    core_send, core_recv, unit_own,
    xa_send, xa_recv, za_send, za_recv, own_a, zb_send, zb_recv, xb_send, xb_recv, own_b, y_send, y_grad, y_recv,
    rel_part, rel_recv, send_sem, recv_sem,
):
    width, rows = left_t.shape
    top = width // 2 // 16 * 16
    edges = src_ref.shape[1]
    negs = neg_ref.shape[1]
    rels = rel_ref.shape[0]
    n_right = edges + negs
    neg_count = edges - 1 + negs
    dom = lax.axis_index("dom")
    row = lax.axis_index("row")
    x, z, c = row // 4, (row // 2) % 2, row % 2

    def row_peer(dx, dz, dc):
        return ((x + dx) % 4) * 4 + ((z + dz) % 2) * 2 + (c + dc) % 2

    core_peer = (dom, row_peer(0, 0, 1))
    z_peer = (dom, row_peer(0, 1, 0))
    x_peers = {dx: (dom, row_peer(dx, 0, 0)) for dx in (1, 2, 3)}
    y_peer = ((dom + dom_size // 2) % dom_size, row)
    if dom_size == 16:
        dom_groups = [
            {j: ((dom + 4 * j) % 16, row) for j in (1, 2, 3)},
            {j: ((dom // 4) * 4 + (dom % 4 + j) % 4, row) for j in (1, 2, 3)},
        ]
    else:
        dom_groups = [{2: y_peer}]
    peers = [core_peer, z_peer, *x_peers.values()]
    for group in dom_groups:
        peers += list(group.values())

    barrier = pltpu.get_barrier_semaphore()
    for peer in peers:
        pl.semaphore_signal(barrier, inc=1, device_id=peer, device_id_type=MESH)

    copies = []

    def send(src, dst, peer):
        k = len(copies)
        copy = pltpu.make_async_remote_copy(
            src_ref=src, dst_ref=dst, send_sem=send_sem.at[k], recv_sem=recv_sem.at[k],
            device_id=peer, device_id_type=MESH,
        )
        copy.start()
        copies.append(copy)
        return copy

    def place(cx, xx, zz):
        return cx * 8 + xx * 2 + zz

    mine = place(c, x, z)

    def positions(ids):
        return ((ids // 128) % 2) * 1024 + (ids // 256) * 128 + ids % 128

    def gather_left_start(rd):
        own = tab_l.at[rd, mine]
        zc = send(own, own, z_peer)
        return zc, {dx: send(own, own, x_peers[dx]) for dx in (2, 1, 3)}

    def gather_right_start(rd):
        own = tab_r.at[rd, mine]
        xc = {dx: send(own, own, x_peers[dx]) for dx in (2, 1, 3)}
        return xc, {0: send(own, own, z_peer)}

    def core_pair(tab, xx):
        part = tab.at[pl.ds(c * 8 + xx * 2, 2)]
        return send(part, part, core_peer)

    def pick_half(tab, ids_ref, out_ref, core, first):
        def tile(start, size):
            ids = ids_ref[:, pl.ds(start, size)] - core * 8 * rows
            hot = (lax.broadcasted_iota(jnp.int32, (8 * rows, size), 0) == ids).astype(F32).astype(BF16)
            table = jnp.concatenate([tab[core * 8 + p] for p in range(8)], axis=1)
            got = dot(table, hot).astype(BF16)
            if not first:
                got = got + out_ref[:, pl.ds(start, size)]
            out_ref[:, pl.ds(start, size)] = got

        tile(0, ids_ref.shape[1])

    def pick_left(rd, core, first=False):
        stage("pick_left", lambda: pick_half(tab_l.at[rd], src_pos, left_rows, core, first))

    def pick_right(rd, core, first=False):
        stage("pick_right", lambda: pick_half(tab_r.at[rd], right_pos, right_rows, core, first))

    def scatter_units(hl_ref, ids_ref, core, xs):
        sub = lax.broadcasted_iota(jnp.int32, (2 * rows, 1), 0)
        inner = core * 8 * rows + jnp.where(sub < rows, sub + (1 - z) * rows, sub - rows + z * rows)
        target = jnp.concatenate([inner + xx * 2 * rows for xx in xs], axis=0)
        hot = (target == ids_ref[...]).astype(F32).astype(BF16)
        both = dot(hl_ref[...], hot, NT)
        return both[:width] + both[width:]

    def adagrad(rows_ref, state_ref, grad):
        state = state_ref[...] + jnp.sum(grad * grad, axis=0, keepdims=True) * (1.0 / width)
        state_ref[...] = state
        new = rows_ref[...] - grad * (STEP_SIZE / (jnp.sqrt(state) + EPSILON))
        rows_ref[...] = new
        return new

    def load():
        left_t[...] = left_ref[...]
        right_t[...] = right_ref[...]
        tab_l[0, mine] = left_t[...].astype(BF16)
        tab_r[0, mine] = right_t[...].astype(BF16)
        left_s[...] = left_state_ref[...]
        right_s[...] = right_state_ref[...]

    stage("load_transpose", load)
    pl.semaphore_wait(barrier, len(peers))

    right_state = gather_right_start(0)
    left_state = gather_left_start(0)

    for rd in range(ROUNDS):
        def indices():
            src_pos[...] = positions(src_ref[rd : rd + 1, :])
            right_pos[:, :edges] = positions(dst_ref[rd : rd + 1, :])
            right_pos[:, edges:] = positions(neg_ref[rd : rd + 1, :])
            rel_hot = (
                lax.broadcasted_iota(jnp.int32, (rels, edges), 0) == relid_ref[rd : rd + 1, :]
            ).astype(F32)
            rel_hot = rel_hot.astype(BF16)
            rel_value = rel_ref[...]
            high = rel_value.astype(BF16)
            rest = rel_value - high.astype(F32)
            mid = rest.astype(BF16)
            low = (rest - mid.astype(F32)).astype(BF16)
            rel_parts = jnp.concatenate([high.astype(F32).T, mid.astype(F32).T, low.astype(F32).T], axis=1)
            rel_rows[...] = dot(rel_parts.astype(BF16), jnp.concatenate([rel_hot] * 3, axis=0))

        stage("indices_relation", indices)

        right_x, right_z = right_state
        left_z, left_x = left_state
        left_cores, right_cores = {}, {}
        left_z.wait_recv()
        got = tab_l.at[rd, place(c, x, 1 - z)]
        left_x2 = {dx: send(got, got, x_peers[dx]) for dx in (2, 1, 3)}
        left_cores[0] = core_pair(tab_l.at[rd], x)
        for dx in (1, 3, 2):
            right_x[dx].wait_recv()
            got = tab_r.at[rd, place(c, (x + 4 - dx) % 4, z)]
            right_z[dx] = send(got, got, z_peer)
        for dx in (0, 1, 3, 2):
            right_z[dx].wait_recv()
            right_cores[dx] = core_pair(tab_r.at[rd], (x + 4 - dx) % 4)
        pick_right(rd, c, True)
        for dx in (1, 3, 2):
            left_x[dx].wait_recv()
            left_x2[dx].wait_recv()
            left_cores[dx] = core_pair(tab_l.at[rd], (x + 4 - dx) % 4)
        for dx in (0, 1, 3, 2):
            right_cores[dx].wait_recv()
        pick_right(rd, 1 - c)

        def transpose():
            right_tr[...] = right_rows[...].astype(F32).T.astype(BF16)

        stage("transpose", transpose)
        pick_left(rd, c, True)
        for dx in (0, 1, 3, 2):
            left_cores[dx].wait_recv()
        pick_left(rd, 1 - c)

        def anchors():
            anchor[...] = (left_rows[...].astype(F32) * rel_rows[...]).astype(BF16)

        stage("anchor", anchors)

        def score_tile(t, carry):
            tile = pl.ds(pl.multiple_of(t * 512, 512), 512)
            scores = dot(right_tr[...], anchor[:, tile])
            weights[:, tile] = ((1.0 / (1.0 + jnp.exp(-scores))) * (1.0 / neg_count)).astype(BF16)
            scores = dot(right_tr[tile, :], anchor[:, tile])
            eye = lax.broadcasted_iota(jnp.int32, (512, 512), 0) == lax.broadcasted_iota(jnp.int32, (512, 512), 1)
            own = -1.0 / (1.0 + jnp.exp(scores))
            rest = weights[tile, tile].astype(F32)
            weights[tile, tile] = jnp.where(eye, own, rest).astype(BF16)
            return carry

        stage("scores", lambda: lax.fori_loop(0, edges // 512, score_tile, 0))

        def grad_right(at, size):
            g = dot(anchor[...], weights[pl.ds(at, size), :], NT)
            high, low = split2(g)
            right_hl[:width, pl.ds(at, size)] = high
            right_hl[width:, pl.ds(at, size)] = low

        stage("grad_right", lambda: grad_right(0, n_right))

        order = (2, 1, 3, 0)

        def scatter(name, hl_ref, ids_ref, base, use, between=lambda k: None):
            sent = {}

            def partner(k):
                def part():
                    units = scatter_units(hl_ref, ids_ref, 1 - c, [(x + order[k + n]) % 4 for n in range(2)])
                    core_send[base + k] = units[:, : 2 * rows]
                    core_send[base + k + 1] = units[:, 2 * rows :]

                stage(name, part)
                for n in (k, k + 1):
                    sent[n] = send(core_send.at[base + n], core_recv.at[base + n], core_peer)

            def own(k):
                def part():
                    unit_own[...] = scatter_units(hl_ref, ids_ref, c, [(x + order[k + n]) % 4 for n in range(2)])

                stage(name, part)
                for n in range(2):
                    sent[k + n].wait_recv()
                    use(k + n, unit_own[:, 2 * rows * n : 2 * rows * (n + 1)] + core_recv[base + k + n])
                between(k)

            partner(0)
            partner(2)
            own(0)
            own(2)

        def sums(side):
            at = rd * 2 + side
            az, ax, bx = {}, {}, {}
            part = {}

            def use(k, unit):
                if order[k]:
                    xa_send[at, k] = unit[:top].astype(BF16)
                    ax[k] = send(xa_send.at[at, k], xa_recv.at[at, k], x_peers[order[k]])
                else:
                    own_a[side] = unit[:top]
                zb_send[at, k] = unit[top:, :rows].astype(BF16)
                az[k] = send(zb_send.at[at, k], zb_recv.at[at, k], z_peer)
                own_b[side * 4 + k] = unit[top:, rows:]

            def rest_on(k):
                az[k].wait_recv()
                total = own_b[side * 4 + k] + zb_recv[at, k].astype(F32)
                if order[k]:
                    xb_send[at, k] = total.astype(BF16)
                    bx[k] = send(xb_send.at[at, k], xb_recv.at[at, k], x_peers[order[k]])
                else:
                    own_b[side * 4 + k] = total

            def top_on():
                total = own_a[side]
                for k in range(3):
                    ax[k].wait_recv()
                    total = total + xa_recv[at, k].astype(F32)
                za_send[at] = total[:, :rows].astype(BF16)
                part["z"] = send(za_send.at[at], za_recv.at[at], z_peer)
                own_a[side, :, rows:] = total[:, rows:]

            def finish():
                total = own_b[side * 4 + 3]
                for k in range(3):
                    bx[k].wait_recv()
                    total = total + xb_recv[at, k].astype(F32)
                part["z"].wait_recv()
                return jnp.concatenate([own_a[side, :, rows:] + za_recv[at].astype(F32), total], axis=0)

            return use, rest_on, top_on, finish

        right_use, right_on, right_top, right_finish = sums(0)
        left_use, left_on, left_top, left_finish = sums(1)
        scatter("scatter_right", right_hl, right_pos, rd * 8, right_use)

        def grad_left_loop(t, carry):
            tile = pl.ds(0, edges)
            g = dot(right_rows[...], weights[:, tile])
            high, low = split2(g * rel_rows[:, tile])
            src_hl[:width, tile] = high
            src_hl[width:, tile] = low
            high, low = split2(g * left_rows[:, tile].astype(F32))
            rel_hl[:width, tile] = high
            rel_hl[width:, tile] = low
            return carry

        stage("grad_left", lambda: grad_left_loop(0, 0))

        def rel_sum():
            hot = lax.broadcasted_iota(jnp.int32, (128, edges), 0) == relid_ref[rd : rd + 1, :]
            both = dot(rel_hl[...], hot.astype(F32).astype(BF16), NT)
            return (both[:width] + both[width:]).T[:rels]

        last = rd == ROUNDS - 1
        rel_wait = None

        def rel_start(slot, at, group):
            return {j: (send(rel_part.at[slot], rel_recv.at[at + n], group[j]), at + n) for n, j in enumerate(group)}

        def rel_step(slot, arriving):
            values = {}
            for j, (copy, at) in arriving.items():
                copy.wait_recv()
                values[j] = rel_recv[at]
            own = rel_part[slot]
            if len(values) == 3:
                total = (own + values[2]) + (values[1] + values[3])
            else:
                (only,) = values.values()
                total = own + only
            rel_part[slot + 1] = total

        if last:
            rel_part[0] = rel_part[5] + rel_sum()
            rel_wait = rel_start(0, 0, {1: core_peer})

        right_on(0)
        right_on(1)

        def between(k):
            nonlocal rel_wait
            if k == 0:
                right_on(2)
                right_on(3)
                if last:
                    rel_step(0, rel_wait)
                    rel_wait = rel_start(1, 1, x_peers)
            if k == 2:
                right_top()

        scatter("scatter_left", src_hl, src_pos, rd * 8 + 4, left_use, between)

        if last:
            rel_step(1, rel_wait)
            rel_wait = rel_start(2, 4, {1: z_peer})
        else:
            rel_part[5] = rel_sum()
        left_on(0)
        left_on(1)
        total = right_finish()
        if last:
            y_grad[...] = total
            to_owner = send(y_grad, y_recv, y_peer)
            rel_step(2, rel_wait)
            rel_wait = rel_start(3, 5, dom_groups[0])
        else:
            new = adagrad(right_t, right_s, total)
            y_send[...] = new.astype(BF16)
            to_holder = send(y_send, tab_r.at[rd + 1, mine], y_peer)
        left_on(2)
        left_on(3)
        left_top()
        if last:
            rel_step(3, rel_wait)
            if len(dom_groups) > 1:
                rel_wait = rel_start(4, 8, dom_groups[1])
        else:
            to_holder.wait_recv()
            right_state = gather_right_start(rd + 1)
        new = adagrad(left_t, left_s, left_finish())
        if not last:
            tab_l[rd + 1, mine] = new.astype(BF16)
            left_state = gather_left_start(rd + 1)
        else:
            left_out[...] = new
            left_state_out[...] = left_s[...]
            to_owner.wait_recv()
            new = adagrad(right_t, right_s, y_recv[...])
            right_out[...] = new
            right_state_out[...] = right_s[...]
            if len(dom_groups) > 1:
                rel_step(4, rel_wait)
            rel_out[...] = rel_part[3 + len(dom_groups)] * rel_scale

    for copy in copies:
        copy.wait_send()


def hand_out(*refs):
    for source, target in zip(refs[:5], refs[5:]):
        target[...] = source[...]


def per_device(
    left_emb, left_state, right_emb, right_state, rel_diag, edge_src, edge_rel, edge_dst, neg_rows
):
    rows, width = left_emb.shape
    edges = edge_src.shape[1]
    negs = neg_rows.shape[2]
    rels = rel_diag.shape[0]
    n_right = edges + negs
    dom_size = lax.axis_size("dom")
    device_count = dom_size * lax.axis_size("row")
    rel_scale = (ROUNDS * edges * device_count) ** (-0.5)
    vmem = pltpu.VMEM
    top = width // 2 // 16 * 16
    shapes = (
        jax.ShapeDtypeStruct((width, rows), F32),
        jax.ShapeDtypeStruct((1, rows), F32),
        jax.ShapeDtypeStruct((width, rows), F32),
        jax.ShapeDtypeStruct((1, rows), F32),
        jax.ShapeDtypeStruct((rels, width), F32),
    )
    outs = pl.pallas_call(
        functools.partial(window_kernel, dom_size, rel_scale),
        out_shape=shapes,
        in_specs=[pl.BlockSpec(memory_space=vmem)] * 9,
        out_specs=tuple([pl.BlockSpec(memory_space=vmem)] * 5),
        scratch_shapes=[
            vmem((width, rows), F32),
            vmem((width, rows), F32),
            vmem((1, rows), F32),
            vmem((1, rows), F32),
            vmem((ROUNDS, 16, width, rows), BF16),
            vmem((ROUNDS, 16, width, rows), BF16),
            vmem((1, edges), jnp.int32),
            vmem((1, n_right), jnp.int32),
            vmem((width, edges), F32),
            vmem((width, edges), BF16),
            vmem((width, edges), BF16),
            vmem((width, n_right), BF16),
            vmem((n_right, width), BF16),
            vmem((n_right, edges), BF16),
            vmem((2 * width, edges), BF16),
            vmem((2 * width, n_right), BF16),
            vmem((2 * width, edges), BF16),
            vmem((ROUNDS * 8, width, 2 * rows), F32),
            vmem((ROUNDS * 8, width, 2 * rows), F32),
            vmem((width, 4 * rows), F32),
            vmem((ROUNDS * 2, 3, top, 2 * rows), BF16),
            vmem((ROUNDS * 2, 3, top, 2 * rows), BF16),
            vmem((ROUNDS * 2, top, rows), BF16),
            vmem((ROUNDS * 2, top, rows), BF16),
            vmem((2, top, 2 * rows), F32),
            vmem((ROUNDS * 2, 4, width - top, rows), BF16),
            vmem((ROUNDS * 2, 4, width - top, rows), BF16),
            vmem((ROUNDS * 2, 3, width - top, rows), BF16),
            vmem((ROUNDS * 2, 3, width - top, rows), BF16),
            vmem((8, width - top, rows), F32),
            vmem((width, rows), BF16),
            vmem((width, rows), F32),
            vmem((width, rows), F32),
            vmem((6, rels, width), F32),
            vmem((11, rels, width), F32),
            pltpu.SemaphoreType.DMA((SEMS,)),
            pltpu.SemaphoreType.DMA((SEMS,)),
        ],
        compiler_params=pltpu.CompilerParams(
            collective_id=0, has_side_effects=True, vmem_limit_bytes=60 * 1024 * 1024
        ),
    )(
        left_emb.T, left_state[None], right_emb.T, right_state[None], rel_diag,
        edge_src, edge_rel, edge_dst, neg_rows.reshape(ROUNDS, negs),
    )
    left_new, left_sum, right_new, right_sum, rel = pl.pallas_call(
        hand_out,
        out_shape=shapes,
        in_specs=[pl.BlockSpec(memory_space=vmem)] * 5,
        out_specs=tuple([pl.BlockSpec(memory_space=vmem)] * 5),
    )(*outs)
    return left_new.T, left_sum.reshape(rows), right_new.T, right_sum.reshape(rows), rel


def solution(mesh):
    placed = (
        P(("dom", "row"), None),
        P(("dom", "row")),
        P(("dom", "row"), None),
        P(("dom", "row")),
        P(),
        P(None, ("dom", "row")),
        P(None, ("dom", "row")),
        P(None, ("dom", "row")),
        P(None, ("dom", "row"), None),
    )
    return jax.shard_map(
        per_device,
        mesh=mesh,
        in_specs=placed,
        out_specs=(
            P(("dom", "row"), None),
            P(("dom", "row")),
            P(("dom", "row"), None),
            P(("dom", "row")),
            P(),
        ),
        check_vma=False,
    )
```

```python
import functools

import jax
import jax.numpy as jnp
from jax import lax
from jax.experimental import pallas as pl
from jax.experimental.pallas import tpu as pltpu
from jax.sharding import PartitionSpec as P

ROUNDS = 2
STEP_SIZE = 0.1
EPSILON = 1e-10
MESH = pl.DeviceIdType.MESH
F32 = jnp.float32
BF16 = jnp.bfloat16
NT = (((1,), (1,)), ((), ()))
NN = (((1,), (0,)), ((), ()))
SEMS = 128


def dot(a, b, dims=NN):
    return lax.dot_general(a, b, dims, preferred_element_type=F32)


def stage(name, fn):
    with jax.named_scope(name):
        fn()


def split2(value):
    high = value.astype(BF16)
    return high, (value - high.astype(F32)).astype(BF16)


def window_kernel(
    dom_size, rel_scale,
    left_ref, left_state_ref, right_ref, right_state_ref, rel_ref, src_ref, relid_ref, dst_ref, neg_ref,
    left_out, left_state_out, right_out, right_state_out, rel_out,
    left_t, right_t, left_s, right_s, tab_l, tab_r, src_pos, right_pos,
    rel_rows, left_rows, anchor, right_rows, right_tr, weights, src_hl, right_hl, rel_hl,
    core_send, core_recv, unit_own,
    xa_send, xa_recv, za_send, za_recv, own_a, zb_send, zb_recv, xb_send, xb_recv, own_b, y_send, y_grad, y_recv,
    rel_part, rel_recv, send_sem, recv_sem,
):
    width, rows = left_t.shape
    top = width // 2 // 16 * 16
    edges = src_ref.shape[1]
    negs = neg_ref.shape[1]
    rels = rel_ref.shape[0]
    n_right = edges + negs
    neg_count = edges - 1 + negs
    dom = lax.axis_index("dom")
    row = lax.axis_index("row")
    x, z, c = row // 4, (row // 2) % 2, row % 2

    def row_peer(dx, dz, dc):
        return ((x + dx) % 4) * 4 + ((z + dz) % 2) * 2 + (c + dc) % 2

    core_peer = (dom, row_peer(0, 0, 1))
    z_peer = (dom, row_peer(0, 1, 0))
    x_peers = {dx: (dom, row_peer(dx, 0, 0)) for dx in (1, 2, 3)}
    y_peer = ((dom + dom_size // 2) % dom_size, row)
    if dom_size == 16:
        dom_groups = [
            {j: ((dom + 4 * j) % 16, row) for j in (1, 2, 3)},
            {j: ((dom // 4) * 4 + (dom % 4 + j) % 4, row) for j in (1, 2, 3)},
        ]
    else:
        dom_groups = [{2: y_peer}]
    peers = [core_peer, z_peer, *x_peers.values()]
    for group in dom_groups:
        peers += list(group.values())

    barrier = pltpu.get_barrier_semaphore()
    for peer in peers:
        pl.semaphore_signal(barrier, inc=1, device_id=peer, device_id_type=MESH)

    copies = []

    def send(src, dst, peer):
        k = len(copies)
        copy = pltpu.make_async_remote_copy(
            src_ref=src, dst_ref=dst, send_sem=send_sem.at[k], recv_sem=recv_sem.at[k],
            device_id=peer, device_id_type=MESH,
        )
        copy.start()
        copies.append(copy)
        return copy

    def place(cx, xx, zz):
        return cx * 8 + xx * 2 + zz

    mine = place(c, x, z)

    def positions(ids):
        return ((ids // 128) % 2) * 1024 + (ids // 256) * 128 + ids % 128

    def gather_left_start(rd):
        own = tab_l.at[rd, mine]
        zc = send(own, own, z_peer)
        return zc, {dx: send(own, own, x_peers[dx]) for dx in (2, 1, 3)}

    def gather_right_start(rd):
        own = tab_r.at[rd, mine]
        xc = {dx: send(own, own, x_peers[dx]) for dx in (2, 1, 3)}
        return xc, {0: send(own, own, z_peer)}

    def core_pair(tab, xx):
        part = tab.at[pl.ds(c * 8 + xx * 2, 2)]
        return send(part, part, core_peer)

    def pick_half(tab, ids_ref, out_ref, core, first):
        def tile(start, size):
            ids = ids_ref[:, pl.ds(start, size)] - core * 8 * rows
            hot = (lax.broadcasted_iota(jnp.int32, (8 * rows, size), 0) == ids).astype(F32).astype(BF16)
            table = jnp.concatenate([tab[core * 8 + p] for p in range(8)], axis=1)
            got = dot(table, hot).astype(BF16)
            if not first:
                got = got + out_ref[:, pl.ds(start, size)]
            out_ref[:, pl.ds(start, size)] = got

        tile(0, ids_ref.shape[1])

    def pick_left(rd, core, first=False):
        stage("pick_left", lambda: pick_half(tab_l.at[rd], src_pos, left_rows, core, first))

    def pick_right(rd, core, first=False):
        stage("pick_right", lambda: pick_half(tab_r.at[rd], right_pos, right_rows, core, first))

    def scatter_units(hl_ref, ids_ref, core, xs):
        sub = lax.broadcasted_iota(jnp.int32, (2 * rows, 1), 0)
        inner = core * 8 * rows + jnp.where(sub < rows, sub + (1 - z) * rows, sub - rows + z * rows)
        target = jnp.concatenate([inner + xx * 2 * rows for xx in xs], axis=0)
        hot = (target == ids_ref[...]).astype(F32).astype(BF16)
        both = dot(hl_ref[...], hot, NT)
        return both[:width] + both[width:]

    def adagrad(rows_ref, state_ref, grad):
        state = state_ref[...] + jnp.sum(grad * grad, axis=0, keepdims=True) * (1.0 / width)
        state_ref[...] = state
        new = rows_ref[...] - grad * (STEP_SIZE / (jnp.sqrt(state) + EPSILON))
        rows_ref[...] = new
        return new

    def load():
        left_t[...] = left_ref[...]
        right_t[...] = right_ref[...]
        tab_l[0, mine] = left_t[...].astype(BF16)
        tab_r[0, mine] = right_t[...].astype(BF16)
        left_s[...] = left_state_ref[...]
        right_s[...] = right_state_ref[...]

    stage("load_transpose", load)
    pl.semaphore_wait(barrier, len(peers))

    right_state = gather_right_start(0)
    left_state = gather_left_start(0)

    for rd in range(ROUNDS):
        def indices():
            src_pos[...] = positions(src_ref[rd : rd + 1, :])
            right_pos[:, :edges] = positions(dst_ref[rd : rd + 1, :])
            right_pos[:, edges:] = positions(neg_ref[rd : rd + 1, :])
            rel_hot = (
                lax.broadcasted_iota(jnp.int32, (rels, edges), 0) == relid_ref[rd : rd + 1, :]
            ).astype(F32)
            rel_hot = rel_hot.astype(BF16)
            rel_value = rel_ref[...]
            high = rel_value.astype(BF16)
            rest = rel_value - high.astype(F32)
            mid = rest.astype(BF16)
            low = (rest - mid.astype(F32)).astype(BF16)
            rel_parts = jnp.concatenate([high.astype(F32).T, mid.astype(F32).T, low.astype(F32).T], axis=1)
            rel_rows[...] = dot(rel_parts.astype(BF16), jnp.concatenate([rel_hot] * 3, axis=0))

        stage("indices_relation", indices)

        right_x, right_z = right_state
        left_z, left_x = left_state
        left_cores, right_cores = {}, {}

        def left_forward():
            left_z.wait_recv()
            got = tab_l.at[rd, place(c, x, 1 - z)]
            left_cores[0] = core_pair(tab_l.at[rd], x)
            return {dx: send(got, got, x_peers[dx]) for dx in (2, 1, 3)}

        def right_forward():
            for dx in (1, 3, 2):
                right_x[dx].wait_recv()
                got = tab_r.at[rd, place(c, (x + 4 - dx) % 4, z)]
                right_z[dx] = send(got, got, z_peer)

        if rd == 0:
            left_x2 = left_forward()
            right_forward()
        else:
            right_forward()
            left_x2 = left_forward()
        for dx in (0, 1, 3, 2):
            right_z[dx].wait_recv()
            right_cores[dx] = core_pair(tab_r.at[rd], (x + 4 - dx) % 4)
        pick_right(rd, c, True)
        for dx in (1, 3, 2):
            left_x[dx].wait_recv()
            left_x2[dx].wait_recv()
            left_cores[dx] = core_pair(tab_l.at[rd], (x + 4 - dx) % 4)
        for dx in (0, 1, 3, 2):
            right_cores[dx].wait_recv()
        pick_right(rd, 1 - c)

        def transpose():
            right_tr[...] = right_rows[...].astype(F32).T.astype(BF16)

        stage("transpose", transpose)
        pick_left(rd, c, True)
        for dx in (0, 1, 3, 2):
            left_cores[dx].wait_recv()
        pick_left(rd, 1 - c)

        def anchors():
            anchor[...] = (left_rows[...].astype(F32) * rel_rows[...]).astype(BF16)

        stage("anchor", anchors)

        def score_tile(t, carry):
            tile = pl.ds(pl.multiple_of(t * 512, 512), 512)
            scores = dot(right_tr[...], anchor[:, tile])
            weights[:, tile] = ((1.0 / (1.0 + jnp.exp(-scores))) * (1.0 / neg_count)).astype(BF16)
            return carry

        def score_all():
            lax.fori_loop(0, edges // 512, score_tile, 0)
            products = anchor[...].astype(F32) * right_rows[:, :edges].astype(F32)
            own = -1.0 / (1.0 + jnp.exp(jnp.sum(products, axis=0, keepdims=True)))
            eye = lax.broadcasted_iota(jnp.int32, (128, 128), 0) == lax.broadcasted_iota(jnp.int32, (128, 128), 1)
            for b in range(edges // 128):
                tile = slice(b * 128, (b + 1) * 128)
                weights[tile, tile] = jnp.where(eye, own[:, tile], weights[tile, tile].astype(F32)).astype(BF16)

        stage("scores", score_all)

        def grad_right(at, size):
            g = dot(anchor[...], weights[pl.ds(at, size), :], NT)
            high, low = split2(g)
            right_hl[:width, pl.ds(at, size)] = high
            right_hl[width:, pl.ds(at, size)] = low

        stage("grad_right", lambda: grad_right(0, n_right))

        order = (2, 1, 3, 0)

        def scatter(name, hl_ref, ids_ref, base, use, between=lambda k: None):
            sent = {}

            def partner(k):
                def part():
                    units = scatter_units(hl_ref, ids_ref, 1 - c, [(x + order[k + n]) % 4 for n in range(2)])
                    core_send[base + k] = units[:, : 2 * rows]
                    core_send[base + k + 1] = units[:, 2 * rows :]

                stage(name, part)
                for n in (k, k + 1):
                    sent[n] = send(core_send.at[base + n], core_recv.at[base + n], core_peer)

            def own(k):
                def part():
                    unit_own[...] = scatter_units(hl_ref, ids_ref, c, [(x + order[k + n]) % 4 for n in range(2)])

                stage(name, part)
                for n in range(2):
                    sent[k + n].wait_recv()
                    use(k + n, unit_own[:, 2 * rows * n : 2 * rows * (n + 1)] + core_recv[base + k + n])
                between(k)

            partner(0)
            partner(2)
            own(0)
            own(2)

        def sums(side):
            at = rd * 2 + side
            az, ax, bx = {}, {}, {}
            part = {}

            def use(k, unit):
                if order[k]:
                    xa_send[at, k] = unit[:top].astype(BF16)
                    ax[k] = send(xa_send.at[at, k], xa_recv.at[at, k], x_peers[order[k]])
                else:
                    own_a[side] = unit[:top]
                zb_send[at, k] = unit[top:, :rows].astype(BF16)
                az[k] = send(zb_send.at[at, k], zb_recv.at[at, k], z_peer)
                own_b[side * 4 + k] = unit[top:, rows:]

            def rest_on(k):
                az[k].wait_recv()
                total = own_b[side * 4 + k] + zb_recv[at, k].astype(F32)
                if order[k]:
                    xb_send[at, k] = total.astype(BF16)
                    bx[k] = send(xb_send.at[at, k], xb_recv.at[at, k], x_peers[order[k]])
                else:
                    own_b[side * 4 + k] = total

            def top_on():
                total = own_a[side]
                for k in range(3):
                    ax[k].wait_recv()
                    total = total + xa_recv[at, k].astype(F32)
                za_send[at] = total[:, :rows].astype(BF16)
                part["z"] = send(za_send.at[at], za_recv.at[at], z_peer)
                own_a[side, :, rows:] = total[:, rows:]

            def finish():
                total = own_b[side * 4 + 3]
                for k in range(3):
                    bx[k].wait_recv()
                    total = total + xb_recv[at, k].astype(F32)
                part["z"].wait_recv()
                return jnp.concatenate([own_a[side, :, rows:] + za_recv[at].astype(F32), total], axis=0)

            return use, rest_on, top_on, finish

        right_use, right_on, right_top, right_finish = sums(0)
        left_use, left_on, left_top, left_finish = sums(1)
        scatter("scatter_right", right_hl, right_pos, rd * 8, right_use)

        def grad_left_loop(t, carry):
            tile = pl.ds(0, edges)
            g = dot(right_rows[...], weights[:, tile])
            high, low = split2(g * rel_rows[:, tile])
            src_hl[:width, tile] = high
            src_hl[width:, tile] = low
            high, low = split2(g * left_rows[:, tile].astype(F32))
            rel_hl[:width, tile] = high
            rel_hl[width:, tile] = low
            return carry

        stage("grad_left", lambda: grad_left_loop(0, 0))

        def rel_sum():
            hot = lax.broadcasted_iota(jnp.int32, (128, edges), 0) == relid_ref[rd : rd + 1, :]
            both = dot(rel_hl[...], hot.astype(F32).astype(BF16), NT)
            return (both[:width] + both[width:]).T[:rels]

        last = rd == ROUNDS - 1
        rel_groups = [{1: core_peer}, *dom_groups, x_peers, {1: z_peer}]
        rel_waits = []

        def rel_start(slot):
            at = sum(len(group) for group in rel_groups[:slot])
            waiting = {}
            for n, j in enumerate(rel_groups[slot]):
                copy = send(rel_part.at[slot], rel_recv.at[at + n], rel_groups[slot][j])
                waiting[j] = (copy, at + n)
            rel_waits.append(waiting)

        def rel_advance():
            slot = len(rel_waits) - 1
            values = {}
            for j, (copy, at) in rel_waits[slot].items():
                copy.wait_recv()
                values[j] = rel_recv[at]
            own = rel_part[slot]
            if len(values) == 3:
                total = (own + values[2]) + (values[1] + values[3])
            else:
                (only,) = values.values()
                total = own + only
            rel_part[slot + 1] = total
            if slot + 1 < len(rel_groups):
                rel_start(slot + 1)

        if last:
            rel_part[0] = rel_part[5] + rel_sum()
            rel_start(0)

        right_on(0)
        right_on(1)

        def between(k):
            if k == 0:
                right_on(2)
                right_on(3)
                if last:
                    rel_advance()
            if k == 2:
                right_top()

        scatter("scatter_left", src_hl, src_pos, rd * 8 + 4, left_use, between)

        if last:
            rel_advance()
        left_on(0)
        left_on(1)
        total = right_finish()
        if last:
            y_grad[...] = total
            to_owner = send(y_grad, y_recv, y_peer)
            rel_advance()
        else:
            new = adagrad(right_t, right_s, total)
            y_send[...] = new.astype(BF16)
            to_holder = send(y_send, tab_r.at[rd + 1, mine], y_peer)
        left_on(2)
        left_on(3)
        left_top()
        if last:
            rel_advance()
        else:
            rel_part[5] = rel_sum()
            to_holder.wait_recv()
            right_state = gather_right_start(rd + 1)
        new = adagrad(left_t, left_s, left_finish())
        if not last:
            tab_l[rd + 1, mine] = new.astype(BF16)
            left_state = gather_left_start(rd + 1)
        else:
            left_out[...] = new
            left_state_out[...] = left_s[...]
            to_owner.wait_recv()
            new = adagrad(right_t, right_s, y_recv[...])
            right_out[...] = new
            right_state_out[...] = right_s[...]
            if len(rel_groups) > 4:
                rel_advance()
            rel_out[...] = rel_part[len(rel_groups)] * rel_scale

    for copy in copies:
        copy.wait_send()


def hand_out(*refs):
    for source, target in zip(refs[:5], refs[5:]):
        target[...] = source[...]


def per_device(
    left_emb, left_state, right_emb, right_state, rel_diag, edge_src, edge_rel, edge_dst, neg_rows
):
    rows, width = left_emb.shape
    edges = edge_src.shape[1]
    negs = neg_rows.shape[2]
    rels = rel_diag.shape[0]
    n_right = edges + negs
    dom_size = lax.axis_size("dom")
    device_count = dom_size * lax.axis_size("row")
    rel_scale = (ROUNDS * edges * device_count) ** (-0.5)
    vmem = pltpu.VMEM
    top = width // 2 // 16 * 16
    shapes = (
        jax.ShapeDtypeStruct((width, rows), F32),
        jax.ShapeDtypeStruct((1, rows), F32),
        jax.ShapeDtypeStruct((width, rows), F32),
        jax.ShapeDtypeStruct((1, rows), F32),
        jax.ShapeDtypeStruct((rels, width), F32),
    )
    outs = pl.pallas_call(
        functools.partial(window_kernel, dom_size, rel_scale),
        out_shape=shapes,
        in_specs=[pl.BlockSpec(memory_space=vmem)] * 9,
        out_specs=tuple([pl.BlockSpec(memory_space=vmem)] * 5),
        scratch_shapes=[
            vmem((width, rows), F32),
            vmem((width, rows), F32),
            vmem((1, rows), F32),
            vmem((1, rows), F32),
            vmem((ROUNDS, 16, width, rows), BF16),
            vmem((ROUNDS, 16, width, rows), BF16),
            vmem((1, edges), jnp.int32),
            vmem((1, n_right), jnp.int32),
            vmem((width, edges), F32),
            vmem((width, edges), BF16),
            vmem((width, edges), BF16),
            vmem((width, n_right), BF16),
            vmem((n_right, width), BF16),
            vmem((n_right, edges), BF16),
            vmem((2 * width, edges), BF16),
            vmem((2 * width, n_right), BF16),
            vmem((2 * width, edges), BF16),
            vmem((ROUNDS * 8, width, 2 * rows), F32),
            vmem((ROUNDS * 8, width, 2 * rows), F32),
            vmem((width, 4 * rows), F32),
            vmem((ROUNDS * 2, 3, top, 2 * rows), BF16),
            vmem((ROUNDS * 2, 3, top, 2 * rows), BF16),
            vmem((ROUNDS * 2, top, rows), BF16),
            vmem((ROUNDS * 2, top, rows), BF16),
            vmem((2, top, 2 * rows), F32),
            vmem((ROUNDS * 2, 4, width - top, rows), BF16),
            vmem((ROUNDS * 2, 4, width - top, rows), BF16),
            vmem((ROUNDS * 2, 3, width - top, rows), BF16),
            vmem((ROUNDS * 2, 3, width - top, rows), BF16),
            vmem((8, width - top, rows), F32),
            vmem((width, rows), BF16),
            vmem((width, rows), F32),
            vmem((width, rows), F32),
            vmem((6, rels, width), F32),
            vmem((11, rels, width), F32),
            pltpu.SemaphoreType.DMA((SEMS,)),
            pltpu.SemaphoreType.DMA((SEMS,)),
        ],
        compiler_params=pltpu.CompilerParams(
            collective_id=0, has_side_effects=True, vmem_limit_bytes=60 * 1024 * 1024
        ),
    )(
        left_emb.T, left_state[None], right_emb.T, right_state[None], rel_diag,
        edge_src, edge_rel, edge_dst, neg_rows.reshape(ROUNDS, negs),
    )
    left_new, left_sum, right_new, right_sum, rel = pl.pallas_call(
        hand_out,
        out_shape=shapes,
        in_specs=[pl.BlockSpec(memory_space=vmem)] * 5,
        out_specs=tuple([pl.BlockSpec(memory_space=vmem)] * 5),
    )(*outs)
    return left_new.T, left_sum.reshape(rows), right_new.T, right_sum.reshape(rows), rel


def solution(mesh):
    placed = (
        P(("dom", "row"), None),
        P(("dom", "row")),
        P(("dom", "row"), None),
        P(("dom", "row")),
        P(),
        P(None, ("dom", "row")),
        P(None, ("dom", "row")),
        P(None, ("dom", "row")),
        P(None, ("dom", "row"), None),
    )
    return jax.shard_map(
        per_device,
        mesh=mesh,
        in_specs=placed,
        out_specs=(
            P(("dom", "row"), None),
            P(("dom", "row")),
            P(("dom", "row"), None),
            P(("dom", "row")),
            P(),
        ),
        check_vma=False,
    )
```
